256 devices in a mesh: pulse: 32 (over z, y), range: 8 (over x, core).
Axes of the slice: x: 4, y: 4, z: 8, core: 2. Of those that a mesh axis runs over, the one named last changes fastest.
Arguments:
- returns_matched: float32 [2, 2048, 2048], P(None, 'pulse', 'range'), may hold values from -6 to 6
- center_wavecount: float32 [1], replicated, may hold values from 2 to 4
- scene_center_distance: float32 [1], replicated, may hold values from 4 to 16
- input_span_offset: int32 [2048, 16], replicated, may hold values from 0 to 128
- filter_choice_list: int32 [16], replicated, may hold values from 0 to 7
- filter_coefficients: float32 [8, 8, 128], replicated, may hold values from -2 to 2
Outputs:
- image: float32 [2, 2048, 2048], P(None, 'pulse', 'range')
The draws below stay inside these ranges and needn't reach their ends.
All inputs are finite; a program needn't handle non-finite values.
Results may differ from the reference program's by a relative error of at most 0.0003.
Values sent between devices are 32-bit elements; how exact they have to be, the bound alone decides.
No kernel may reach another device: no remote copies, remote signals or barrier semaphores. Data moves between devices by JAX's collectives and lax.ppermute only.
A program may use at most 64 MiB of HBM per device.

```python
import math
import jax
import jax.numpy as jnp
from jax import lax

P_DEV = 64
BLK = 128
TAPS = 8
NW = 8
NP = 2048
NR = 2048
WIN = 256
NB = 16


def set_ends(values, stream_key, least, largest):
    spot = [jax.random.randint(jax.random.fold_in(stream_key, axis), (), 0, length) for axis, length in enumerate(values.shape)]
    main_axis = values.shape.index(max(values.shape))
    neighbour = spot[:main_axis] + [(spot[main_axis] + 1) % values.shape[main_axis]] + spot[main_axis + 1:]
    return values.at[tuple(spot)].set(least).at[tuple(neighbour)].set(largest)


def level_of(own_key, shape, shards, smallest, largest):
    def one(axis_at, blocks):
        steps = jax.random.uniform(jax.random.fold_in(jax.random.fold_in(own_key, 6), axis_at), (blocks,), jnp.float32, smallest / len(shards), largest / len(shards))
        return jnp.repeat(jnp.exp(steps), shape[axis_at] // blocks).reshape((-1,) + (1,) * (len(shape) - axis_at - 1))

    factor_of = one(*shards[0])
    for cut in shards[1:]:
        factor_of = factor_of * one(*cut)
    return factor_of


def gaussian(stream_key, extent, deviation, most, cuts=(), kind=jnp.bfloat16):
    gain = level_of(stream_key, extent, cuts, -0.22, 0.18) if cuts else 1.0
    entries = jax.random.normal(stream_key, extent, jnp.float32) * deviation * gain
    return jnp.minimum(jnp.maximum(entries, -most), most).astype(kind)


def setup_inputs(seed: int = 0) -> dict:
    arg_keys = jax.random.split(jax.random.key(seed), 7)
    return {
        "returns_matched": gaussian(arg_keys[0], (2, NP, NR), 1.0, 6.0, ((1, 32), (2, 8)), jnp.float32),
        "center_wavecount": jnp.clip(jax.random.uniform(arg_keys[1], (1,), jnp.float32, 2.0, 4.0), 2.0, 4.0),
        "scene_center_distance": jnp.clip(jax.random.uniform(arg_keys[2], (1,), jnp.float32, 4.0, 16.0), 4.0, 16.0),
        "input_span_offset": set_ends(jax.random.randint(arg_keys[3], (NP, NB), 0, BLK + 1), jax.random.fold_in(arg_keys[3], 1), 0, BLK).astype(jnp.int32),
        "filter_choice_list": set_ends(jax.random.randint(arg_keys[4], (NB,), 0, NW), jax.random.fold_in(arg_keys[4], 1), 0, NW - 1).astype(jnp.int32),
        "filter_coefficients": gaussian(arg_keys[5], (NW, TAPS, BLK), TAPS ** -0.5, 2.0, (), jnp.float32),
    }


def matched_filter_argument(spatial_horizontal_lines, spatial_vertical_lines, center_wavecount, scene_center_distance):
    doppler_variable = ((spatial_horizontal_lines + NP // 2) % NP - NP // 2).astype(jnp.float32) / NP
    slant_spatial_variable = ((spatial_vertical_lines + NR // 2) % NR - NR // 2).astype(jnp.float32) / NR
    return 2.0 * math.pi * scene_center_distance[0] * jnp.sqrt((center_wavecount[0] + slant_spatial_variable[None, :]) ** 2 - 0.25 * doppler_variable[:, None] ** 2)

def reference(returns_matched, center_wavecount, scene_center_distance, input_span_offset, filter_choice_list, filter_coefficients):
    spectrum = jnp.fft.fft2(lax.complex(returns_matched[0], returns_matched[1]))
    spec_re = jnp.real(spectrum)
    spec_im = jnp.imag(spectrum)
    stretch = (BLK - TAPS) // (NW - 1)
    inside = jnp.arange(BLK, dtype=jnp.int32)
    offsets = inside[None, :] * (BLK + stretch * filter_choice_list[:, None]) // BLK
    column_off = offsets.reshape(NR)
    vertical_element = jnp.arange(NR, dtype=jnp.int32)
    block_base = vertical_element // BLK * BLK + column_off
    column_taps = jnp.transpose(filter_coefficients[filter_choice_list], (1, 0, 2)).reshape(TAPS, NR)

    def rows_fn(pieces):
        first_row, rows_re, rows_im, row_shifts = pieces
        spatial_horizontal_lines = first_row + jnp.arange(P_DEV, dtype=jnp.int32)
        turning_radians = matched_filter_argument(spatial_horizontal_lines, vertical_element, center_wavecount, scene_center_distance)
        cosine = jnp.cos(turning_radians)
        sine_val = jnp.sin(turning_radians)
        turned_re = rows_re * cosine - rows_im * sine_val
        turned_im = rows_re * sine_val + rows_im * cosine
        turned_re = jnp.pad(turned_re, ((0, 0), (0, WIN)))
        turned_im = jnp.pad(turned_im, ((0, 0), (0, WIN)))
        source_base = block_base[None, :] + jnp.repeat(row_shifts, BLK, axis=1)
        summed_re = jnp.zeros((P_DEV, NR), turned_re.dtype)
        summed_im = jnp.zeros((P_DEV, NR), turned_re.dtype)
        for tap_index in range(TAPS):
            source = (source_base + tap_index).astype(jnp.int32)
            summed_re = summed_re + column_taps[tap_index][None, :] * jnp.take_along_axis(turned_re, source, axis=1)
            summed_im = summed_im + column_taps[tap_index][None, :] * jnp.take_along_axis(turned_im, source, axis=1)
        return (summed_re, summed_im)
    groups_total = NP // P_DEV
    first_rows = jnp.arange(groups_total, dtype=jnp.int32) * P_DEV
    focused_re, focused_im = lax.map(rows_fn, (first_rows, spec_re.reshape(groups_total, P_DEV, NR), spec_im.reshape(groups_total, P_DEV, NR), input_span_offset.reshape(groups_total, P_DEV, NB)))
    focused = lax.complex(focused_re.reshape(NP, NR), focused_im.reshape(NP, NR))
    result = jnp.fft.ifft2(focused)
    return jnp.stack([jnp.real(result), jnp.imag(result)]).astype(jnp.float32)
```

```python
import functools
import math

import jax
import jax.numpy as jnp
import ml_dtypes
import numpy as np
from jax import lax
from jax.experimental import pallas as pl
from jax.experimental.pallas import tpu as pltpu
from jax.sharding import PartitionSpec as P

BLK = 128
TAPS = 8
NW = 8
N = 2048
ROWS = 256
FEW = 8
LANES = 128
STRETCH = (BLK - TAPS) // (NW - 1)


def halves(table):
    high = table.astype(np.float32).astype(ml_dtypes.bfloat16)
    low = (table - high.astype(np.float64)).astype(np.float32).astype(ml_dtypes.bfloat16)
    return high, low


@functools.lru_cache(maxsize=None)
def tables():
    steps = np.arange(ROWS)
    angle = 2.0 * math.pi / ROWS * (steps[:, None] * steps[None, :] % ROWS)
    cosine, sine = np.cos(angle), np.sin(angle)
    perm = steps % 8 * 32 + steps // 8
    found = {
        "plain": halves(np.concatenate([cosine, sine])),
        "range_in": halves(np.concatenate([cosine[:, perm], sine[:, perm]])),
        "range_out": halves(np.concatenate([cosine[perm], sine[perm]])),
    }
    lane = np.arange(LANES)
    part, mid, low = lane // 64, lane // 8 % 8, lane % 8
    for name, digit in (("mid", mid), ("low", low)):
        turn = 2.0 * math.pi / N * (steps[:, None] * digit[None, :])
        sign = np.where(part == 0, 1.0, -1.0)
        found["tw_" + name] = (
            np.cos(turn).astype(np.float32),
            (np.sin(turn) * sign[None, :]).astype(np.float32),
        )
        other = low if name == "mid" else mid
        same = other[:, None] == other[None, :]
        eighth = 2.0 * math.pi / FEW * (digit[:, None] * digit[None, :] % FEW)
        for way, orient in (("fwd", -1.0), ("inv", 1.0)):
            real, imag = np.cos(eighth), orient * np.sin(eighth)
            mixed = np.where(
                part[:, None] == part[None, :],
                real,
                np.where(part[:, None] < part[None, :], imag, -imag),
            )
            found[f"few_{name}_{way}"] = halves(np.where(same, mixed, 0.0))
    return found


def split(x):
    high = x.astype(jnp.bfloat16)
    low = (x - high.astype(jnp.float32)).astype(jnp.bfloat16)
    return high, low


def dot(left, right):
    return jnp.dot(left, right, preferred_element_type=jnp.float32)


def left_dot(high, low, x):
    x_high, x_low = split(x)
    both = dot(high, jnp.concatenate([x_high, x_low], axis=1))
    return both[:, :LANES] + both[:, LANES:] + dot(low, x_high)


def right_dot(x, high, low):
    x_high, x_low = split(x)
    return dot(x_high, high) + (dot(x_low, high) + dot(x_high, low))


def swapped(x):
    return pltpu.roll(x, LANES // 2, 1)


def sign_row(orient):
    lane = lax.broadcasted_iota(jnp.int32, (1, LANES), 1)
    return jnp.where(lane < LANES // 2, -orient, orient).astype(jnp.float32)


def rows_dft(high_ref, low_ref, x, orient):
    both = left_dot(high_ref[...], low_ref[...], x)
    return both[:ROWS] + swapped(both[ROWS:]) * sign_row(orient)


def forward(x, lh, ll, tc, ts, gh, gl):
    y = rows_dft(lh, ll, x, -1.0)
    z = y * tc[...] + swapped(y) * ts[...]
    return right_dot(z, gh[...], gl[...])


def inverse(x, lh, ll, tc, ts, gh, gl):
    y = right_dot(x, gh[...], gl[...])
    z = y * tc[...] - swapped(y) * ts[...]
    return rows_dft(lh, ll, z, 1.0)


def exchange(parts):
    group = lax.broadcasted_iota(jnp.int32, parts[0].shape, 1) // 8
    parts = list(parts)
    for bit in range(4):
        step = 1 << bit
        keep = group // step % 2 == 0
        for first in range(16):
            if first & step:
                continue
            a, b = parts[first], parts[first + step]
            parts[first] = jnp.where(keep, a, pltpu.roll(b, 8 * step, 1))
            parts[first + step] = jnp.where(keep, pltpu.roll(a, LANES - 8 * step, 1), b)
    return parts


def pack_kernel(x_ref, out_ref, held):
    for half in range(2):
        held[half] = x_ref[:, :, half * LANES : (half + 1) * LANES]
    parts = []
    for q in range(16):
        part, low = divmod(q, 8)
        parts.append(
            jnp.concatenate(
                [
                    held[half, part, pl.ds(low, 8, stride=8), :] for half in range(2)
                ],
                axis=0,
            )
        )
    for g, one in enumerate(exchange(parts)):
        for half in range(2):
            out_ref[half * 16 + g] = one[half * 8 : half * 8 + 8]


def unpack_kernel(x_ref, out_ref, held):
    parts = [jnp.concatenate([x_ref[g], x_ref[16 + g]], axis=0) for g in range(16)]
    for q, one in enumerate(exchange(parts)):
        part, low = divmod(q, 8)
        for half in range(2):
            held[half, part, pl.ds(low, 8, stride=8), :] = one[half * 8 : half * 8 + 8]
    for half in range(2):
        out_ref[:, :, half * LANES : (half + 1) * LANES] = held[half]


def azimuth_kernel(x_ref, lh, ll, tc, ts, gh, gl, out_ref):
    x = x_ref[...].reshape(ROWS, LANES)
    out_ref[...] = forward(x, lh, ll, tc, ts, gh, gl)


def azimuth_back_kernel(x_ref, lh, ll, tc, ts, gh, gl, out_ref):
    y = inverse(x_ref[...], lh, ll, tc, ts, gh, gl) * (1.0 / (N * N))
    out_ref[...] = y.reshape(32, 8, LANES)


def prepare_kernel(
    rank_ref, count_ref, distance_ref, choice_ref, shift_ref, coef_ref,
    cos_ref, sin_ref, high_ref, low_ref, lane_ref,
):
    lane = lax.broadcasted_iota(jnp.int32, (ROWS, LANES), 1)
    row = lax.broadcasted_iota(jnp.int32, (ROWS, LANES), 0)
    kx = rank_ref[0] + ROWS * (lane // 8 % 8)
    kr = row + ROWS * (lane % 8)
    fx = ((kx + N // 2) % N - N // 2).astype(jnp.float32) / N
    fr = ((kr + N // 2) % N - N // 2).astype(jnp.float32) / N
    turns = distance_ref[0] * jnp.sqrt((count_ref[0] + fr) ** 2 - 0.25 * fx**2)
    radians = (turns - jnp.round(turns)) * (2.0 * math.pi)
    cos_ref[...] = jnp.cos(radians)
    sin_ref[...] = jnp.sin(radians) * sign_row(1.0)
    few_lane = lax.broadcasted_iota(jnp.int32, (8, LANES), 1)
    few_row = lax.broadcasted_iota(jnp.int32, (8, LANES), 0)
    own = few_lane // 8 % 8 == few_row
    col = lax.broadcasted_iota(jnp.int32, (16, LANES), 0)
    col_lane = lax.broadcasted_iota(jnp.int32, (16, LANES), 1)
    starts = shift_ref[...].astype(jnp.float32).astype(jnp.bfloat16)
    for half in range(2):
        pick = (col == 2 * (col_lane % 8) + half).astype(jnp.float32).astype(jnp.bfloat16)
        spread = jnp.where(own, dot(starts, pick), 0.0)
        lane_ref[half : half + 1, :] = jnp.sum(spread, axis=0, keepdims=True).astype(jnp.int32)
        one = lax.broadcasted_iota(jnp.int32, (1, LANES), 1) % 8
        chosen = jnp.zeros((1, LANES), jnp.int32)
        for j in range(8):
            chosen = jnp.where(one == j, choice_ref[2 * j + half], chosen)
        lane_ref[2 + half : 3 + half, :] = chosen
    lane_ref[4:8, :] = jnp.zeros((4, LANES), jnp.int32)
    columns = jnp.transpose(coef_ref[...])
    inside = lax.broadcasted_iota(jnp.int32, (BLK, 2 * BLK), 0)
    window = lax.broadcasted_iota(jnp.int32, (BLK, 2 * BLK), 1)
    for d in range(NW):
        ahead = window - inside * (BLK + STRETCH * d) // BLK
        band = jnp.zeros((BLK, 2 * BLK), jnp.float32)
        for t in range(TAPS):
            band = jnp.where(ahead == t, columns[:, d * TAPS + t : d * TAPS + t + 1], band)
        high, low = split(band)
        high_ref[d * BLK : (d + 1) * BLK, :] = high
        low_ref[d * BLK : (d + 1) * BLK, :] = low


def stolt(turned, bh, bl, lane_ref):
    lane = lax.broadcasted_iota(jnp.int32, (1, LANES), 1)
    following = jnp.where(lane % 8 == 7, 0.0, pltpu.roll(turned, LANES - 1, 1))
    long = jnp.concatenate([turned, following], axis=0)
    highs, lows = [], []
    for half in range(2):
        based = long[half * BLK : half * BLK + 3 * BLK]
        starts = lane_ref[half : half + 1, :]
        for bit in reversed(range(8)):
            step = 1 << bit
            flagged = starts // step % 2 == 1
            length = 2 * BLK + (step if step >= 8 else 8 if step > 1 else 0)
            if step < 8:
                moved = pltpu.roll(based, based.shape[0] - step, 0)
            else:
                moved = jnp.concatenate([based[step:], based[:step]], axis=0)
            based = jnp.where(flagged, moved[:length], based[:length])
        high, low = split(based)
        highs.append(high)
        lows.append(low)
    high, low = jnp.concatenate(highs, axis=1), jnp.concatenate(lows, axis=1)
    chosen = jnp.concatenate([lane_ref[2:3, :], lane_ref[3:4, :]], axis=1)
    result = jnp.zeros((BLK, 2 * LANES), jnp.float32)
    for d in range(NW):
        own = pl.ds(d * BLK, BLK)
        one = dot(bh[own, :], high) + (dot(bh[own, :], low) + dot(bl[own, :], high))
        result = jnp.where(chosen == d, one, result)
    return jnp.concatenate([result[:, :LANES], result[:, LANES:]], axis=0)


def range_kernel(
    x_ref, lh, ll, tc, ts, gh, gl, cos_ref, sin_ref, bh, bl, lane_ref, kh, kl, hh, hl, out_ref
):
    lines = forward(x_ref[...], lh, ll, tc, ts, gh, gl)
    turned = lines * cos_ref[...] + swapped(lines) * sin_ref[...]
    focused = stolt(turned, bh, bl, lane_ref)
    out_ref[...] = inverse(focused, kh, kl, tc, ts, hh, hl)


VMEM = pl.BlockSpec(memory_space=pltpu.VMEM)
SMEM = pl.BlockSpec(memory_space=pltpu.SMEM)
HELD = [pltpu.VMEM((2, 2, 64, LANES), jnp.float32)]


def call(kernel, shapes, *args, scalars=0, flops=10**8, scratch=()):
    return pl.pallas_call(
        kernel,
        out_shape=shapes,
        in_specs=[SMEM] * scalars + [VMEM] * (len(args) - scalars),
        out_specs=jax.tree.map(lambda _: VMEM, shapes),
        scratch_shapes=scratch,
        compiler_params=pltpu.CompilerParams(vmem_limit_bytes=32 * 2**20),
        cost_estimate=pl.CostEstimate(flops=flops, bytes_accessed=2**20, transcendentals=0),
    )(*args)


def f32(*shape):
    return jax.ShapeDtypeStruct(shape, jnp.float32)


def local(returns, center, distance, starts, choices, coefficients):
    known = tables()
    rank = lax.axis_index("pulse") * 8 + lax.axis_index("range")
    own_starts = lax.dynamic_index_in_dim(starts.reshape(8, ROWS, 16), rank, 1, keepdims=False)
    cosine, sine, band_high, band_low, lane_rows = call(
        prepare_kernel,
        (
            f32(ROWS, LANES),
            f32(ROWS, LANES),
            jax.ShapeDtypeStruct((NW * BLK, 2 * BLK), jnp.bfloat16),
            jax.ShapeDtypeStruct((NW * BLK, 2 * BLK), jnp.bfloat16),
            jax.ShapeDtypeStruct((8, LANES), jnp.int32),
        ),
        rank.reshape(1).astype(jnp.int32), center, distance, choices,
        own_starts, coefficients.reshape(NW * TAPS, BLK),
        scalars=4,
    )
    x = call(pack_kernel, f32(32, 8, LANES), returns, scratch=HELD)
    x = lax.all_to_all(x, "pulse", 0, 0, tiled=True)
    x = call(
        azimuth_kernel, f32(ROWS, LANES), x,
        *known["plain"], *known["tw_mid"], *known["few_mid_fwd"],
    )
    x = lax.all_to_all(x.reshape(ROWS, 1, LANES), ("pulse", "range"), 0, 0, tiled=True)
    x = call(
        range_kernel, f32(ROWS, LANES), x.reshape(ROWS, LANES),
        *known["range_in"], *known["tw_low"], *known["few_low_fwd"],
        cosine, sine, band_high, band_low, lane_rows,
        *known["range_out"], *known["few_low_inv"],
    )
    x = lax.all_to_all(x.reshape(ROWS, 1, LANES), ("pulse", "range"), 0, 0, tiled=True)
    x = call(
        azimuth_back_kernel, f32(32, 8, LANES), x.reshape(ROWS, LANES),
        *known["plain"], *known["tw_mid"], *known["few_mid_inv"],
    )
    x = lax.all_to_all(x, "pulse", 0, 0, tiled=True)
    return call(unpack_kernel, f32(2, 64, 256), x, scratch=HELD)


def solution(mesh):
    placed = (P(None, "pulse", "range"), P(), P(), P(), P(), P())
    return jax.shard_map(
        local, mesh=mesh, in_specs=placed, out_specs=P(None, "pulse", "range"), check_vma=False
    )
```

```python
import math

import jax
import jax.numpy as jnp
import ml_dtypes
import numpy as np
from jax import lax
from jax.experimental import pallas as pl
from jax.experimental.pallas import tpu as pltpu
from jax.sharding import PartitionSpec as P

BLK = 128
TAPS = 8
NW = 8
N = 2048
ROWS = 256
QUARTER = 64
FEW = 8
LANES = 128
STRETCH = (BLK - TAPS) // (NW - 1)


def halves(table):
    high = table.astype(np.float32).astype(ml_dtypes.bfloat16)
    low = (table - high.astype(np.float64)).astype(np.float32).astype(ml_dtypes.bfloat16)
    return high, low


def tables():
    steps = np.arange(QUARTER)
    angle = 2.0 * math.pi / QUARTER * (steps[:, None] * steps[None, :] % QUARTER)
    high, low = halves(np.concatenate([np.cos(angle), np.sin(angle)]))
    lane = np.arange(LANES)
    part, mid, last = lane // 64, lane // 8 % 8, lane % 8
    eighth = 2.0 * math.pi / FEW * (mid[:, None] * last[None, :] % FEW)
    cosine, sine = np.cos(eighth), np.sin(eighth)
    step = part[None, :] - part[:, None]
    few = np.where(step == 0, cosine, np.where(step > 0, -sine, sine))
    few = np.where(last[:, None] == mid[None, :], few, 0.0)
    few_high, few_low = halves(np.concatenate([few, few.T], axis=1))
    matrices = np.concatenate([np.concatenate([high, high, low, low], axis=1), few_high, few_low])
    outer = 2.0 * math.pi / N * (np.arange(ROWS)[:, None] * mid[None, :])
    inner = np.concatenate([2.0 * math.pi / ROWS * steps * r for r in range(1, 4)])
    inner = np.broadcast_to(inner[:, None], (3 * QUARTER, LANES))
    sign = np.where(part == 0, 1.0, -1.0)[None, :]
    turns = [np.cos(outer), np.sin(outer) * sign, np.cos(inner), np.sin(inner) * sign]
    return matrices, np.concatenate(turns).astype(np.float32)


def split(x):
    high = x.astype(jnp.bfloat16)
    low = (x - high.astype(jnp.float32)).astype(jnp.bfloat16)
    return high, low


def dot(left, right):
    return jnp.dot(left, right, preferred_element_type=jnp.float32)


def swapped(x):
    return pltpu.roll(x, LANES // 2, 1)


def sign_row(orient):
    lane = lax.broadcasted_iota(jnp.int32, (1, LANES), 1)
    return jnp.where(lane < LANES // 2, -orient, orient).astype(jnp.float32)


def times_i(x, orient):
    return swapped(x) * sign_row(orient)


def turned_by(x, cosine, sine, orient):
    other = swapped(x) * sine
    return x * cosine + other if orient < 0 else x * cosine - other


def butterfly(y, orient):
    even, gap = y[0] + y[2], y[0] - y[2]
    odd, side = y[1] + y[3], times_i(y[1] - y[3], orient)
    return [even + odd, gap + side, even - odd, gap - side]


def quarter_dft(blocks, matrix_ref, orient):
    high, low = split(jnp.concatenate(blocks, axis=1))
    both = dot(matrix_ref[: 2 * QUARTER], jnp.concatenate([high, low, high, low], axis=0))
    found = []
    for r in range(4):
        across = slice(r * LANES, (r + 1) * LANES)
        found.append(both[:QUARTER, across] + times_i(both[QUARTER:, across], orient))
    return found


def quarter_turns(y, turn_ref, orient):
    found = [y[0]]
    for r in range(1, 4):
        cosine = turn_ref[pl.ds(2 * ROWS + (r - 1) * QUARTER, QUARTER)]
        sine = turn_ref[pl.ds(2 * ROWS + (r + 2) * QUARTER, QUARTER)]
        found.append(turned_by(y[r], cosine, sine, orient))
    return found


def few_dft(x, matrix_ref, way):
    high, low = split(x)
    across = pl.ds(way * LANES, LANES)
    table_high = matrix_ref[pl.ds(LANES, LANES), across]
    table_low = matrix_ref[pl.ds(2 * LANES, LANES), across]
    return dot(
        jnp.concatenate([high, low, high, low], axis=1),
        jnp.concatenate([table_high, table_high, table_low, table_low], axis=0),
    )


def forward(x_ref, matrix_ref, turn_ref):
    y = [x_ref[pl.ds(r, QUARTER, stride=4), :] for r in range(4)]
    y = quarter_turns(quarter_dft(y, matrix_ref, -1.0), turn_ref, -1.0)
    z = jnp.concatenate(butterfly(y, -1.0), axis=0)
    return few_dft(turned_by(z, turn_ref[:ROWS], turn_ref[ROWS : 2 * ROWS], -1.0), matrix_ref, 0)


def inverse(x, matrix_ref, turn_ref, out_ref, scale=1.0):
    z = turned_by(few_dft(x, matrix_ref, 1), turn_ref[:ROWS], turn_ref[ROWS : 2 * ROWS], 1.0)
    y = butterfly([z[q * QUARTER : (q + 1) * QUARTER] for q in range(4)], 1.0)
    y = quarter_dft(quarter_turns(y, turn_ref, 1.0), matrix_ref, 1.0)
    for r in range(4):
        out_ref[pl.ds(r, QUARTER, stride=4), :] = y[r] * scale


def exchange(parts):
    group = lax.broadcasted_iota(jnp.int32, parts[0].shape, 1) // 8
    parts = list(parts)
    for bit in range(4):
        step = 1 << bit
        keep = group // step % 2 == 0
        for first in range(16):
            if first & step:
                continue
            a, b = parts[first], parts[first + step]
            parts[first] = jnp.where(keep, a, pltpu.roll(b, 8 * step, 1))
            parts[first + step] = jnp.where(keep, pltpu.roll(a, LANES - 8 * step, 1), b)
    return parts


def first_kernel(out_ref):
    out_ref[...] = jnp.zeros_like(out_ref)


def pack_kernel(count_ref, distance_ref, x_ref, first_ref, choice_ref, out_ref, held):
    for half in range(2):
        held[half] = x_ref[:, :, half * LANES : (half + 1) * LANES]
        parts = [held[half, q // 8, pl.ds(q % 8, 8, stride=8), :] for q in range(16)]
        for g, one in enumerate(exchange(parts)):
            out_ref[half * 16 + g] = one


def unpack_kernel(x_ref, out_ref, held, sems):
    copies = []
    for half in range(2):
        for q, one in enumerate(exchange([x_ref[half * 16 + g] for g in range(16)])):
            held[half, q // 8, pl.ds(q % 8, 8, stride=8), :] = one
        copies.append(
            pltpu.make_async_copy(
                held.at[half], out_ref.at[:, :, pl.ds(half * LANES, LANES)], sems.at[half]
            )
        )
        copies[half].start()
    for copy in copies:
        copy.wait()


def azimuth_kernel(x_ref, matrix_ref, turn_ref, out_ref):
    out_ref[...] = forward(x_ref, matrix_ref, turn_ref)


def azimuth_back_kernel(x_ref, matrix_ref, turn_ref, out_ref):
    inverse(x_ref[...], matrix_ref, turn_ref, out_ref, 1.0 / (N * N))


def own_rank():
    return lax.axis_index("range") * 32 + lax.axis_index("pulse")


def polynomial(u, terms):
    total = jnp.full_like(u, terms[-1])
    for term in reversed(terms[:-1]):
        total = total * u + term
    return total


def turn_tables(turns):
    halves_count = jnp.round(2.0 * turns)
    rest = turns - 0.5 * halves_count
    odd = halves_count - 2.0 * jnp.floor(0.5 * halves_count)
    sign = 1.0 - 2.0 * odd
    turn = 2.0 * math.pi
    even_terms = [(-1) ** k * turn ** (2 * k) / math.factorial(2 * k) for k in range(8)]
    odd_terms = [(-1) ** k * turn ** (2 * k + 1) / math.factorial(2 * k + 1) for k in range(7)]
    square = rest * rest
    return sign * polynomial(square, even_terms), sign * rest * polynomial(square, odd_terms)


def both_parts(table):
    first = lax.broadcasted_iota(jnp.int32, (1, LANES), 1) < LANES // 2
    other = swapped(table)
    upper, lower = jnp.where(first, table, other), jnp.where(first, other, table)
    return jnp.concatenate([upper, lower], axis=0)


def half_rows(lane):
    row = lax.broadcasted_iota(jnp.int32, (BLK, LANES), 0)
    return row + jnp.where(lane >= LANES // 2, BLK, 0)


def phase_tables(rank, count, distance):
    lane = lax.broadcasted_iota(jnp.int32, (1, LANES), 1)
    kx = rank + ROWS * (lane // 8 % 8)
    kr = half_rows(lane) + ROWS * (lane % 8)
    fx = jnp.where(kx >= N // 2, kx - N, kx).astype(jnp.float32) * (1.0 / N)
    fr = jnp.where(kr >= N // 2, kr - N, kr).astype(jnp.float32) * (1.0 / N)
    cosine, sine = turn_tables(distance * jnp.sqrt((count + fr) ** 2 - 0.25 * fx**2))
    return both_parts(cosine), both_parts(sine) * sign_row(1.0)


def lane_rows(rank, starts_ref, choice_ref):
    lane = lax.broadcasted_iota(jnp.int32, (1, LANES), 1)
    row = lax.broadcasted_iota(jnp.int32, (16, LANES), 0)
    tile = rank // LANES * LANES
    own = lane == rank - tile
    spread = jnp.zeros((16, LANES), jnp.float32)
    for k in range(FEW):
        at = pl.multiple_of(tile + ROWS * k, LANES)
        some = starts_ref[:, pl.ds(at, LANES)].astype(jnp.float32)
        one = jnp.sum(jnp.where(own, some, 0.0), axis=1, keepdims=True)
        spread = jnp.where(lane // 8 % 8 == k, one, spread)
    starts, chosen = [], []
    for half in range(2):
        mine = jnp.where(row == 2 * (lane % 8) + half, spread, 0.0)
        starts.append(jnp.sum(mine, axis=0, keepdims=True).astype(jnp.int32))
        picked = jnp.zeros((1, LANES), jnp.float32)
        for j in range(FEW):
            at = 2 * j + half
            picked = jnp.where(lane % 8 == j, choice_ref[:1, at : at + 1], picked)
        chosen.append(picked.astype(jnp.int32))
    return starts, jnp.concatenate(chosen, axis=1)


def write_bands(coef_ref, high_ref, low_ref):
    coef = coef_ref[...]
    columns = jnp.transpose(jnp.concatenate([coef, coef], axis=0))
    lane = lax.broadcasted_iota(jnp.int32, (16, LANES), 1)
    row = lax.broadcasted_iota(jnp.int32, (16, LANES), 0)
    for d in range(NW):
        slope = BLK + STRETCH * d
        for g in range(BLK // 16):
            least = 16 * g * slope // BLK
            most = (16 * g + 15) * slope // BLK + TAPS - 1
            start = (row + 16 * g) * slope // BLK
            rows = pl.ds(d * BLK + 16 * g, 16)
            for tile in range(2):
                across = pl.ds(tile * LANES, LANES)
                if least >= (tile + 1) * LANES or most < tile * LANES:
                    high_ref[rows, across] = jnp.zeros((16, LANES), jnp.bfloat16)
                    low_ref[rows, across] = jnp.zeros((16, LANES), jnp.bfloat16)
                    continue
                ahead = lane + tile * LANES - start
                inside = (ahead >= 0) & (ahead < TAPS)
                at = jnp.where(inside, ahead, 0) + d * TAPS
                taken = jnp.take_along_axis(
                    columns[16 * g : 16 * g + 16], at, axis=1, mode="promise_in_bounds"
                )
                high, low = split(jnp.where(inside, taken, 0.0))
                high_ref[rows, across] = high
                low_ref[rows, across] = low


def stolt(turned, bh, bl, all_starts, chosen):
    lane = lax.broadcasted_iota(jnp.int32, (1, LANES), 1)
    following = jnp.where(lane % 8 == 7, 0.0, pltpu.roll(turned, LANES - 1, 1))
    long = jnp.concatenate([turned, following], axis=0)
    highs, lows = [], []
    for half in range(2):
        based = long[half * BLK : half * BLK + 3 * BLK]
        starts = all_starts[half]
        for bit in reversed(range(8)):
            step = 1 << bit
            flagged = starts // step % 2 == 1
            length = 2 * BLK + (step if step >= 8 else 8 if step > 1 else 0)
            if step < 8:
                moved = pltpu.roll(based, based.shape[0] - step, 0)
            else:
                moved = jnp.concatenate([based[step:], based[:step]], axis=0)
            based = jnp.where(flagged, moved[:length], based[:length])
        high, low = split(based)
        highs.append(high)
        lows.append(low)
    high, low = jnp.concatenate(highs, axis=1), jnp.concatenate(lows, axis=1)
    windows = jnp.concatenate([high, low, high], axis=0)
    result = jnp.zeros((BLK, 2 * LANES), jnp.float32)
    for d in range(NW):
        own = pl.ds(d * BLK, BLK)
        band = jnp.concatenate([bh[own, :], bh[own, :], bl[own, :]], axis=1)
        result = jnp.where(chosen == d, dot(band, windows), result)
    return jnp.concatenate([result[:, :LANES], result[:, LANES:]], axis=0)


def range_kernel(
    count_ref, distance_ref, x_ref, matrix_ref, turn_ref, choice_ref, starts_ref, coef_ref,
    out_ref, bh, bl,
):
    rank = own_rank()
    lines = forward(x_ref, matrix_ref, turn_ref)
    cosine, sine = phase_tables(rank, count_ref[0], distance_ref[0])
    turned = lines * cosine + swapped(lines) * sine
    write_bands(coef_ref, bh, bl)
    starts, chosen = lane_rows(rank, starts_ref, choice_ref)
    focused = stolt(turned, bh, bl, starts, chosen)
    inverse(focused, matrix_ref, turn_ref, out_ref)


VMEM = pl.BlockSpec(memory_space=pltpu.VMEM)
SMEM = pl.BlockSpec(memory_space=pltpu.SMEM)
HBM = pl.BlockSpec(memory_space=pltpu.HBM)
HELD = pltpu.VMEM((2, 2, 64, LANES), jnp.float32)


def call(kernel, shapes, *args, scalars=0, outs=VMEM, scratch=()):
    return pl.pallas_call(
        kernel,
        out_shape=shapes,
        in_specs=[SMEM] * scalars + [VMEM] * (len(args) - scalars),
        out_specs=jax.tree.map(lambda _: outs, shapes),
        scratch_shapes=scratch,
        compiler_params=pltpu.CompilerParams(vmem_limit_bytes=32 * 2**20),
        cost_estimate=pl.CostEstimate(flops=10**10, bytes_accessed=2**20, transcendentals=0),
    )(*args)


def f32(*shape):
    return jax.ShapeDtypeStruct(shape, jnp.float32)


def bf16(*shape):
    return jax.ShapeDtypeStruct(shape, jnp.bfloat16)


def local(returns, center, distance, starts, choices, coefficients):
    whole = ("range", "pulse")
    known = tables()
    choices = choices.astype(jnp.float32).reshape(1, 16)
    first = call(first_kernel, f32(8, LANES))
    x = call(
        pack_kernel, f32(32, 8, LANES), center, distance, returns, first, choices,
        scalars=2, scratch=[HELD],
    )
    x = lax.all_to_all(x, "pulse", 0, 0, tiled=True)
    x = call(azimuth_kernel, f32(ROWS, LANES), x.reshape(ROWS, LANES), *known)
    x = lax.all_to_all(x.reshape(ROWS, 1, LANES), whole, 0, 0, tiled=True)
    x = call(
        range_kernel, f32(ROWS, LANES), center, distance, x.reshape(ROWS, LANES), *known,
        choices, starts.T, coefficients.reshape(NW * TAPS, BLK),
        scalars=2,
        scratch=[pltpu.VMEM((NW * BLK, 2 * BLK), jnp.bfloat16)] * 2,
    )
    x = lax.all_to_all(x.reshape(ROWS, 1, LANES), whole, 0, 0, tiled=True)
    x = call(azimuth_back_kernel, f32(ROWS, LANES), x.reshape(ROWS, LANES), *known)
    x = lax.all_to_all(x.reshape(32, 8, LANES), "pulse", 0, 0, tiled=True)
    return call(
        unpack_kernel, f32(2, 64, 256), x, outs=HBM,
        scratch=[HELD, pltpu.SemaphoreType.DMA((2,))],
    )


def solution(mesh):
    placed = (P(None, "pulse", "range"), P(), P(), P(), P(), P())
    return jax.shard_map(
        local, mesh=mesh, in_specs=placed, out_specs=P(None, "pulse", "range"), check_vma=False
    )
```

```python
import math

import jax
import jax.numpy as jnp
import ml_dtypes
import numpy as np
from jax import lax
from jax.experimental import pallas as pl
from jax.experimental.pallas import tpu as pltpu
from jax.sharding import PartitionSpec as P

BLK = 128
TAPS = 8
NW = 8
N = 2048
ROWS = 256
QUARTER = 64
FEW = 8
LANES = 128
STRETCH = (BLK - TAPS) // (NW - 1)


def halves(table):
    high = table.astype(np.float32).astype(ml_dtypes.bfloat16)
    low = (table - high.astype(np.float64)).astype(np.float32).astype(ml_dtypes.bfloat16)
    return high, low


FIRST, LAST = slice(0, 128), slice(128, 192)
INTO, INTO_I, BACK, BACK_I = (slice(at, at + 128) for at in range(192, 704, 128))


def tables():
    steps = np.arange(QUARTER)
    angle = 2.0 * math.pi / QUARTER * (steps[:, None] * steps[None, :] % QUARTER)
    cosine, sine = np.cos(angle), np.sin(angle)
    high, low = halves(np.concatenate([cosine, -sine]))
    first = np.concatenate([high, high, low, low], axis=1)
    last = np.concatenate(halves(np.concatenate([cosine, sine], axis=1)), axis=1)
    lane = np.arange(LANES)
    part, mid, low_digit = lane // 64, lane // 8 % 8, lane % 8
    eighth = 2.0 * math.pi / FEW * (mid[:, None] * low_digit[None, :] % FEW)
    cosine, sine = np.cos(eighth), np.sin(eighth)
    step = part[None, :] - part[:, None]
    few = np.where(step == 0, cosine, np.where(step > 0, -sine, sine))
    few = np.where(low_digit[:, None] == mid[None, :], few, 0.0)
    times_i = np.where(lane[:, None] % 64 == lane[None, :] % 64, step, 0).astype(np.float64)
    parts = []
    for one in (few, few @ times_i, few.T, few.T @ times_i):
        large = np.where(np.abs(one) > 0.9, np.round(one), 0.0)
        small = np.where(large == 0, np.sign(np.round(2 * one)), 0.0)
        parts.append(np.concatenate([large, small], axis=1))
    whole = [part.astype(ml_dtypes.bfloat16) for part in parts]
    matrices = np.concatenate([first, last, *whole])
    outer = 2.0 * math.pi / N * (np.arange(ROWS)[:, None] * mid[None, :])
    inner = np.concatenate([2.0 * math.pi / ROWS * steps * r for r in range(1, 4)])
    inner = np.broadcast_to(inner[:, None], (3 * QUARTER, LANES))
    turns = [np.cos(outer), np.sin(outer), np.cos(inner), np.sin(inner)]
    return matrices, np.concatenate(turns).astype(np.float32)


def split(x):
    high = x.astype(jnp.bfloat16)
    low = (x - high.astype(jnp.float32)).astype(jnp.bfloat16)
    return high, low


def dot(left, right):
    return jnp.dot(left, right, preferred_element_type=jnp.float32)


def swapped(x):
    return pltpu.roll(x, LANES // 2, 1)


def turned_by(pair, cosine, sine):
    a, b = pair
    return a * cosine + b * sine, b * cosine - a * sine


def butterfly(y):
    (a0, b0), (a1, b1), (a2, b2), (a3, b3) = y
    even, gap = (a0 + a2, b0 + b2), (a0 - a2, b0 - b2)
    odd, side = (a1 + a3, b1 + b3), (b1 - b3, a3 - a1)
    return [
        (even[0] + odd[0], even[1] + odd[1]),
        (gap[0] + side[0], gap[1] + side[1]),
        (even[0] - odd[0], even[1] - odd[1]),
        (gap[0] - side[0], gap[1] - side[1]),
    ]


def quarter_turns(y, turn_ref):
    found = [y[0]]
    for r in range(1, 4):
        cosine = turn_ref[pl.ds(2 * ROWS + (r - 1) * QUARTER, QUARTER)]
        sine = turn_ref[pl.ds(2 * ROWS + (r + 2) * QUARTER, QUARTER)]
        found.append(turned_by(y[r], cosine, sine))
    return found


def few_dft(x, table):
    both = dot(jnp.concatenate(x, axis=1), jnp.concatenate(table, axis=0))
    return both[:, :LANES] + both[:, LANES:] * math.sqrt(0.5)


def forward(x_ref, matrix_ref, turn_ref, sides=False):
    x = jnp.concatenate([x_ref[pl.ds(r, QUARTER, stride=4), :] for r in range(4)], axis=1)
    high, low = split(x)
    both = dot(matrix_ref[FIRST], jnp.concatenate([high, low, high, low], axis=0))
    y = []
    for r in range(4):
        one = both[:, r * LANES : (r + 1) * LANES]
        y.append((one[:QUARTER], one[QUARTER:]))
    y = butterfly(quarter_turns(y, turn_ref))
    pair = [jnp.concatenate([one[at] for one in y], axis=0) for at in range(2)]
    a, b = turned_by(pair, turn_ref[:ROWS], turn_ref[ROWS : 2 * ROWS])
    into, into_i = matrix_ref[INTO], matrix_ref[INTO_I]
    if not sides:
        return few_dft([*split(a), *split(b)], [into, into, into_i, into_i])
    lane = lax.broadcasted_iota(jnp.int32, (1, LANES), 1)
    pieces = split(a + swapped(b * jnp.where(lane < LANES // 2, 1.0, -1.0)))
    return few_dft(pieces, [into, into]), few_dft(pieces, [into_i, into_i])


def inverse(x, matrix_ref, turn_ref, out_ref, scale=1.0):
    pieces = split(x)
    back, back_i = matrix_ref[BACK], matrix_ref[BACK_I]
    pair = few_dft(pieces, [back, back]), few_dft(pieces, [back_i, back_i])
    pair = turned_by(pair, turn_ref[:ROWS], turn_ref[ROWS : 2 * ROWS])
    y = [tuple(one[q * QUARTER : (q + 1) * QUARTER] for one in pair) for q in range(4)]
    y = quarter_turns(butterfly(y), turn_ref)
    y = jnp.concatenate([jnp.concatenate(one, axis=0) for one in y], axis=1)
    high, low = split(y)
    last = matrix_ref[LAST]
    wide = jnp.concatenate([last[:, :LANES], last[:, :LANES], last[:, LANES:]], axis=1)
    found = dot(wide, jnp.concatenate([high, low, high], axis=0))
    for r in range(4):
        one = found[:, r * LANES : (r + 1) * LANES]
        out_ref[pl.ds(r, QUARTER, stride=4), :] = one * scale


def exchange(parts):
    group = lax.broadcasted_iota(jnp.int32, parts[0].shape, 1) // 8
    parts = list(parts)
    for step in (1, 4):
        digit = group // step % 4
        masks = [digit == j for j in range(4)]
        for first in range(16):
            if first // step % 4:
                continue
            old = [parts[first + step * i] for i in range(4)]
            for i in range(4):
                one = old[i]
                for j in range(4):
                    if j != i:
                        moved = pltpu.roll(old[j], (j - i) * 8 * step % LANES, 1)
                        one = jnp.where(masks[j], moved, one)
                parts[first + step * i] = one
    return parts


def first_kernel(out_ref):
    out_ref[...] = jnp.zeros_like(out_ref)


def pack_kernel(count_ref, distance_ref, x_ref, first_ref, choice_ref, out_ref, held):
    for half in range(2):
        held[half] = x_ref[:, :, half * LANES : (half + 1) * LANES]
    parts = []
    for q in range(16):
        some = [held[half, q // 8, pl.ds(q % 8, 8, stride=8), :] for half in range(2)]
        parts.append(jnp.concatenate(some, axis=0))
    for g, one in enumerate(exchange(parts)):
        for half in range(2):
            out_ref[half * 16 + g] = one[half * 8 : half * 8 + 8]


def unpack_kernel(x_ref, out_ref, held, sems):
    parts = [jnp.concatenate([x_ref[g], x_ref[16 + g]], axis=0) for g in range(16)]
    copies = []
    for q, one in enumerate(exchange(parts)):
        for half in range(2):
            held[half, q // 8, pl.ds(q % 8, 8, stride=8), :] = one[half * 8 : half * 8 + 8]
        if q % 8 == 7:
            for half in range(2):
                copies.append(
                    pltpu.make_async_copy(
                        held.at[half, q // 8],
                        out_ref.at[q // 8, :, pl.ds(half * LANES, LANES)],
                        sems.at[q // 8 * 2 + half],
                    )
                )
                copies[-1].start()
    for copy in copies:
        copy.wait()


def azimuth_kernel(x_ref, matrix_ref, turn_ref, out_ref):
    out_ref[...] = forward(x_ref, matrix_ref, turn_ref)


def azimuth_back_kernel(x_ref, matrix_ref, turn_ref, out_ref):
    inverse(x_ref[...], matrix_ref, turn_ref, out_ref, 1.0 / (N * N))


def own_rank():
    return lax.axis_index("range") * 32 + lax.axis_index("pulse")


def polynomial(u, terms):
    total = jnp.full_like(u, terms[-1])
    for term in reversed(terms[:-1]):
        total = total * u + term
    return total


def turn_tables(turns):
    halves_count = jnp.round(2.0 * turns)
    rest = turns - 0.5 * halves_count
    odd = halves_count - 2.0 * jnp.floor(0.5 * halves_count)
    sign = 1.0 - 2.0 * odd
    turn = 2.0 * math.pi
    even_terms = [(-1) ** k * turn ** (2 * k) / math.factorial(2 * k) for k in range(7)]
    odd_terms = [(-1) ** k * turn ** (2 * k + 1) / math.factorial(2 * k + 1) for k in range(6)]
    square = rest * rest
    return sign * polynomial(square, even_terms), sign * rest * polynomial(square, odd_terms)


def both_parts(table):
    first = lax.broadcasted_iota(jnp.int32, (1, LANES), 1) < LANES // 2
    other = swapped(table)
    upper, lower = jnp.where(first, table, other), jnp.where(first, other, table)
    return jnp.concatenate([upper, lower], axis=0)


def half_rows(lane):
    row = lax.broadcasted_iota(jnp.int32, (BLK, LANES), 0)
    return row + jnp.where(lane >= LANES // 2, BLK, 0)


def phase_tables(rank, count, distance):
    lane = lax.broadcasted_iota(jnp.int32, (1, LANES), 1)
    kx = rank + ROWS * (lane // 8 % 8)
    kr = half_rows(lane) + ROWS * (lane % 8)
    fx = jnp.where(kx >= N // 2, kx - N, kx).astype(jnp.float32) * (1.0 / N)
    fr = jnp.where(kr >= N // 2, kr - N, kr).astype(jnp.float32) * (1.0 / N)
    cosine, sine = turn_tables(distance * jnp.sqrt((count + fr) ** 2 - 0.25 * fx**2))
    return both_parts(cosine), both_parts(sine)


def lane_rows(rank, starts_ref, choice_ref):
    lane = lax.broadcasted_iota(jnp.int32, (1, LANES), 1)
    row = lax.broadcasted_iota(jnp.int32, (16, LANES), 0)
    tile = rank // LANES * LANES
    own = lane == rank - tile
    spread = jnp.zeros((16, LANES), jnp.float32)
    for k in range(FEW):
        at = pl.multiple_of(tile + ROWS * k, LANES)
        some = starts_ref[:, pl.ds(at, LANES)].astype(jnp.float32)
        one = jnp.sum(jnp.where(own, some, 0.0), axis=1, keepdims=True)
        spread = jnp.where(lane // 8 % 8 == k, one, spread)
    starts, chosen = [], []
    for half in range(2):
        mine = jnp.where(row == 2 * (lane % 8) + half, spread, 0.0)
        starts.append(jnp.sum(mine, axis=0, keepdims=True).astype(jnp.int32))
        picked = jnp.zeros((1, LANES), jnp.float32)
        for j in range(FEW):
            at = 2 * j + half
            picked = jnp.where(lane % 8 == j, choice_ref[:1, at : at + 1], picked)
        chosen.append(picked.astype(jnp.int32))
    return starts, jnp.concatenate(chosen, axis=1)


PER_LANE = lax.GatherDimensionNumbers(
    offset_dims=(),
    collapsed_slice_dims=(0,),
    start_index_map=(0,),
    operand_batching_dims=(1,),
    start_indices_batching_dims=(1,),
)
PER_ROW = lax.GatherDimensionNumbers(
    offset_dims=(),
    collapsed_slice_dims=(1,),
    start_index_map=(1,),
    operand_batching_dims=(0,),
    start_indices_batching_dims=(0,),
)


def write_bands(coef_ref, high_ref, low_ref):
    coef = coef_ref[...]
    columns = jnp.transpose(jnp.concatenate([coef, coef], axis=0))
    lane = lax.broadcasted_iota(jnp.int32, (16, LANES), 1)
    row = lax.broadcasted_iota(jnp.int32, (16, LANES), 0)
    for d in range(NW):
        slope = BLK + STRETCH * d
        sloped = row * slope
        for g in range(BLK // 16):
            least = 16 * g * slope // BLK
            most = (16 * g + 15) * slope // BLK + TAPS - 1
            whole, rest = divmod(16 * g * slope, BLK)
            start = (sloped + rest) >> 7
            rows = pl.ds(d * BLK + 16 * g, 16)
            for tile in range(2):
                across = pl.ds(tile * LANES, LANES)
                if least >= (tile + 1) * LANES or most < tile * LANES:
                    high_ref[rows, across] = jnp.zeros((16, LANES), jnp.bfloat16)
                    low_ref[rows, across] = jnp.zeros((16, LANES), jnp.bfloat16)
                    continue
                ahead = (lane + (tile * LANES - whole)) - start
                tap = ahead & (TAPS - 1)
                taken = lax.gather(
                    columns[16 * g : 16 * g + 16],
                    (tap | (d * TAPS))[:, :, None],
                    PER_ROW,
                    (1, 1),
                    mode=lax.GatherScatterMode.PROMISE_IN_BOUNDS,
                )
                high, low = split(jnp.where(tap == ahead, taken, 0.0))
                high_ref[rows, across] = high
                low_ref[rows, across] = low


def stolt(turned, bh, bl, all_starts, chosen):
    lane = lax.broadcasted_iota(jnp.int32, (1, LANES), 1)
    following = jnp.where(lane % 8 == 7, 0.0, pltpu.roll(turned, LANES - 1, 1))
    long = jnp.concatenate([turned, following], axis=0)
    highs, lows = [], []
    for half in range(2):
        based = long[half * BLK : half * BLK + 3 * BLK]
        starts = all_starts[half]
        for bit in reversed(range(3, 8)):
            step = 1 << bit
            flagged = (starts >> bit) & 1 == 1
            moved = jnp.concatenate([based[step:], based[:step]], axis=0)
            based = jnp.where(flagged, moved, based)[: 2 * BLK + step]
        fine = lax.broadcasted_iota(jnp.int32, (8, LANES), 0) + (starts & 7)
        groups = [
            lax.gather(
                based[8 * g : 8 * g + 8],
                (fine & 7)[:, :, None],
                PER_LANE,
                (1, 1),
                mode=lax.GatherScatterMode.PROMISE_IN_BOUNDS,
            )
            for g in range(2 * BLK // 8 + 1)
        ]
        here = fine < 8
        based = jnp.concatenate(
            [jnp.where(here, groups[g], groups[g + 1]) for g in range(2 * BLK // 8)], axis=0
        )
        high, low = split(based)
        highs.append(high)
        lows.append(low)
    high, low = jnp.concatenate(highs, axis=1), jnp.concatenate(lows, axis=1)
    windows = jnp.concatenate([high, low, high], axis=0)
    result = jnp.zeros((BLK, 2 * LANES), jnp.float32)
    for d in range(NW):
        own = pl.ds(d * BLK, BLK)
        band = jnp.concatenate([bh[own, :], bh[own, :], bl[own, :]], axis=1)
        result = jnp.where(chosen == d, dot(band, windows), result)
    return jnp.concatenate([result[:, :LANES], result[:, LANES:]], axis=0)


def range_kernel(
    count_ref, distance_ref, x_ref, matrix_ref, turn_ref, choice_ref, starts_ref, coef_ref,
    out_ref, bh, bl,
):
    rank = own_rank()
    lines, side = forward(x_ref, matrix_ref, turn_ref, sides=True)
    cosine, sine = phase_tables(rank, count_ref[0], distance_ref[0])
    turned = lines * cosine + side * sine
    write_bands(coef_ref, bh, bl)
    starts, chosen = lane_rows(rank, starts_ref, choice_ref)
    focused = stolt(turned, bh, bl, starts, chosen)
    inverse(focused, matrix_ref, turn_ref, out_ref)


VMEM = pl.BlockSpec(memory_space=pltpu.VMEM)
SMEM = pl.BlockSpec(memory_space=pltpu.SMEM)
HBM = pl.BlockSpec(memory_space=pltpu.HBM)
HELD = pltpu.VMEM((2, 2, 64, LANES), jnp.float32)


def call(kernel, shapes, *args, scalars=0, outs=VMEM, scratch=()):
    return pl.pallas_call(
        kernel,
        out_shape=shapes,
        in_specs=[SMEM] * scalars + [VMEM] * (len(args) - scalars),
        out_specs=jax.tree.map(lambda _: outs, shapes),
        scratch_shapes=scratch,
        compiler_params=pltpu.CompilerParams(vmem_limit_bytes=32 * 2**20),
        cost_estimate=pl.CostEstimate(flops=10**10, bytes_accessed=2**20, transcendentals=0),
    )(*args)


def f32(*shape):
    return jax.ShapeDtypeStruct(shape, jnp.float32)


def bf16(*shape):
    return jax.ShapeDtypeStruct(shape, jnp.bfloat16)


def local(returns, center, distance, starts, choices, coefficients):
    whole = ("range", "pulse")
    known = tables()
    choices = choices.astype(jnp.float32).reshape(1, 16)
    first = call(first_kernel, f32(8, LANES))
    x = call(
        pack_kernel, f32(32, 8, LANES), center, distance, returns, first, choices,
        scalars=2, scratch=[HELD],
    )
    x = lax.all_to_all(x, "pulse", 0, 0, tiled=True)
    x = call(azimuth_kernel, f32(ROWS, LANES), x.reshape(ROWS, LANES), *known)
    x = lax.all_to_all(x.reshape(ROWS, 1, LANES), whole, 0, 0, tiled=True)
    x = call(
        range_kernel, f32(ROWS, LANES), center, distance, x.reshape(ROWS, LANES), *known,
        choices, starts.T, coefficients.reshape(NW * TAPS, BLK),
        scalars=2,
        scratch=[pltpu.VMEM((NW * BLK, 2 * BLK), jnp.bfloat16)] * 2,
    )
    x = lax.all_to_all(x.reshape(ROWS, 1, LANES), whole, 0, 0, tiled=True)
    x = call(azimuth_back_kernel, f32(ROWS, LANES), x.reshape(ROWS, LANES), *known)
    x = lax.all_to_all(x.reshape(32, 8, LANES), "pulse", 0, 0, tiled=True)
    return call(
        unpack_kernel, f32(2, 64, 256), x, outs=HBM,
        scratch=[HELD, pltpu.SemaphoreType.DMA((4,))],
    )


def solution(mesh):
    placed = (P(None, "pulse", "range"), P(), P(), P(), P(), P())
    return jax.shard_map(
        local, mesh=mesh, in_specs=placed, out_specs=P(None, "pulse", "range"), check_vma=False
    )
```

```python
import math

import jax
import jax.numpy as jnp
import ml_dtypes
import numpy as np
from jax import lax
from jax.experimental import pallas as pl
from jax.experimental.pallas import tpu as pltpu
from jax.sharding import PartitionSpec as P

BLK = 128
TAPS = 8
NW = 8
N = 2048
ROWS = 256
QUARTER = 64
FEW = 8
LANES = 128
STRETCH = (BLK - TAPS) // (NW - 1)


def halves(table):
    high = table.astype(np.float32).astype(ml_dtypes.bfloat16)
    low = (table - high.astype(np.float64)).astype(np.float32).astype(ml_dtypes.bfloat16)
    return high, low


FIRST, LAST = slice(0, 128), slice(128, 192)
INTO, INTO_I, BACK, BACK_I = (slice(at, at + 128) for at in range(192, 704, 128))


def tables():
    steps = np.arange(QUARTER)
    angle = 2.0 * math.pi / QUARTER * (steps[:, None] * steps[None, :] % QUARTER)
    cosine, sine = np.cos(angle), np.sin(angle)
    high, low = halves(np.concatenate([cosine, -sine]))
    first = np.concatenate([high, high, low, low], axis=1)
    last = np.concatenate(halves(np.concatenate([cosine, sine], axis=1)), axis=1)
    lane = np.arange(LANES)
    part, mid, low_digit = lane // 64, lane // 8 % 8, lane % 8
    eighth = 2.0 * math.pi / FEW * (mid[:, None] * low_digit[None, :] % FEW)
    cosine, sine = np.cos(eighth), np.sin(eighth)
    step = part[None, :] - part[:, None]
    few = np.where(step == 0, cosine, np.where(step > 0, -sine, sine))
    few = np.where(low_digit[:, None] == mid[None, :], few, 0.0)
    times_i = np.where(lane[:, None] % 64 == lane[None, :] % 64, step, 0).astype(np.float64)
    parts = []
    for one in (few, few @ times_i, few.T, few.T @ times_i):
        large = np.where(np.abs(one) > 0.9, np.round(one), 0.0)
        small = np.where(large == 0, np.sign(np.round(2 * one)), 0.0)
        parts.append(np.concatenate([large, small], axis=1))
    whole = [part.astype(ml_dtypes.bfloat16) for part in parts]
    matrices = np.concatenate([first, last, *whole])
    outer = 2.0 * math.pi / N * (np.arange(ROWS)[:, None] * mid[None, :])
    inner = np.concatenate([2.0 * math.pi / ROWS * steps * r for r in range(1, 4)])
    inner = np.broadcast_to(inner[:, None], (3 * QUARTER, LANES))
    turns = [np.cos(outer), np.sin(outer), np.cos(inner), np.sin(inner)]
    return matrices, np.concatenate(turns).astype(np.float32)


def split(x):
    high = x.astype(jnp.bfloat16)
    low = (x - high.astype(jnp.float32)).astype(jnp.bfloat16)
    return high, low


def dot(left, right):
    return jnp.dot(left, right, preferred_element_type=jnp.float32)


def swapped(x):
    return pltpu.roll(x, LANES // 2, 1)


def turned_by(pair, cosine, sine):
    a, b = pair
    return a * cosine + b * sine, b * cosine - a * sine


def butterfly(y):
    (a0, b0), (a1, b1), (a2, b2), (a3, b3) = y
    even, gap = (a0 + a2, b0 + b2), (a0 - a2, b0 - b2)
    odd, side = (a1 + a3, b1 + b3), (b1 - b3, a3 - a1)
    return [
        (even[0] + odd[0], even[1] + odd[1]),
        (gap[0] + side[0], gap[1] + side[1]),
        (even[0] - odd[0], even[1] - odd[1]),
        (gap[0] - side[0], gap[1] - side[1]),
    ]


def quarter_turns(y, turn_ref):
    found = [y[0]]
    for r in range(1, 4):
        cosine = turn_ref[pl.ds(2 * ROWS + (r - 1) * QUARTER, QUARTER)]
        sine = turn_ref[pl.ds(2 * ROWS + (r + 2) * QUARTER, QUARTER)]
        found.append(turned_by(y[r], cosine, sine))
    return found


def few_dft(x, table):
    both = dot(jnp.concatenate(x, axis=1), jnp.concatenate(table, axis=0))
    return both[:, :LANES] + both[:, LANES:] * math.sqrt(0.5)


def forward(x_ref, matrix_ref, turn_ref, sides=False):
    x = jnp.concatenate([x_ref[pl.ds(r, QUARTER, stride=4), :] for r in range(4)], axis=1)
    high, low = split(x)
    both = dot(matrix_ref[FIRST], jnp.concatenate([high, low, high, low], axis=0))
    y = []
    for r in range(4):
        one = both[:, r * LANES : (r + 1) * LANES]
        y.append((one[:QUARTER], one[QUARTER:]))
    y = butterfly(quarter_turns(y, turn_ref))
    pair = [jnp.concatenate([one[at] for one in y], axis=0) for at in range(2)]
    a, b = turned_by(pair, turn_ref[:ROWS], turn_ref[ROWS : 2 * ROWS])
    into, into_i = matrix_ref[INTO], matrix_ref[INTO_I]
    if not sides:
        return few_dft([*split(a), *split(b)], [into, into, into_i, into_i])
    lane = lax.broadcasted_iota(jnp.int32, (1, LANES), 1)
    pieces = split(a + swapped(b * jnp.where(lane < LANES // 2, 1.0, -1.0)))
    return few_dft(pieces, [into, into]), few_dft(pieces, [into_i, into_i])


def inverse(x, matrix_ref, turn_ref, out_ref, scale=1.0):
    pieces = split(x)
    back, back_i = matrix_ref[BACK], matrix_ref[BACK_I]
    pair = few_dft(pieces, [back, back]), few_dft(pieces, [back_i, back_i])
    pair = turned_by(pair, turn_ref[:ROWS], turn_ref[ROWS : 2 * ROWS])
    y = [tuple(one[q * QUARTER : (q + 1) * QUARTER] for one in pair) for q in range(4)]
    y = quarter_turns(butterfly(y), turn_ref)
    y = jnp.concatenate([jnp.concatenate(one, axis=0) for one in y], axis=1)
    high, low = split(y)
    last = matrix_ref[LAST]
    wide = jnp.concatenate([last[:, :LANES], last[:, :LANES], last[:, LANES:]], axis=1)
    found = dot(wide, jnp.concatenate([high, low, high], axis=0))
    for r in range(4):
        one = found[:, r * LANES : (r + 1) * LANES]
        out_ref[pl.ds(r, QUARTER, stride=4), :] = one * scale


def exchange(parts):
    group = lax.broadcasted_iota(jnp.int32, parts[0].shape, 1) // 8
    parts = list(parts)
    for step in (1, 4):
        digit = group // step % 4
        masks = [digit == j for j in range(4)]
        for first in range(16):
            if first // step % 4:
                continue
            old = [parts[first + step * i] for i in range(4)]
            for i in range(4):
                one = old[i]
                for j in range(4):
                    if j != i:
                        moved = pltpu.roll(old[j], (j - i) * 8 * step % LANES, 1)
                        one = jnp.where(masks[j], moved, one)
                parts[first + step * i] = one
    return parts


def pack_kernel(x_ref, out_ref, held):
    for half in range(2):
        held[half] = x_ref[:, :, half * LANES : (half + 1) * LANES]
    parts = []
    for q in range(16):
        some = [held[half, q // 8, pl.ds(q % 8, 8, stride=8), :] for half in range(2)]
        parts.append(jnp.concatenate(some, axis=0))
    for g, one in enumerate(exchange(parts)):
        for half in range(2):
            out_ref[half * 16 + g] = one[half * 8 : half * 8 + 8]


def unpack_kernel(x_ref, out_ref, held, sems):
    parts = [jnp.concatenate([x_ref[g], x_ref[16 + g]], axis=0) for g in range(16)]
    copies = []
    for q, one in enumerate(exchange(parts)):
        for half in range(2):
            held[half, q // 8, pl.ds(q % 8, 8, stride=8), :] = one[half * 8 : half * 8 + 8]
        if q % 8 == 7:
            for half in range(2):
                copies.append(
                    pltpu.make_async_copy(
                        held.at[half, q // 8],
                        out_ref.at[q // 8, :, pl.ds(half * LANES, LANES)],
                        sems.at[q // 8 * 2 + half],
                    )
                )
                copies[-1].start()
    for copy in copies:
        copy.wait()


def azimuth_kernel(x_ref, matrix_ref, turn_ref, lane_ref, out_ref):
    out_ref[...] = forward(x_ref, matrix_ref, turn_ref)


def azimuth_back_kernel(x_ref, matrix_ref, turn_ref, out_ref):
    inverse(x_ref[...], matrix_ref, turn_ref, out_ref, 1.0 / (N * N))


def own_rank():
    return lax.axis_index("range") * 32 + lax.axis_index("pulse")


def polynomial(u, terms):
    total = jnp.full_like(u, terms[-1])
    for term in reversed(terms[:-1]):
        total = total * u + term
    return total


def turn_tables(turns):
    halves_count = jnp.round(2.0 * turns)
    rest = turns - 0.5 * halves_count
    odd = halves_count - 2.0 * jnp.floor(0.5 * halves_count)
    sign = 1.0 - 2.0 * odd
    turn = 2.0 * math.pi
    even_terms = [(-1) ** k * turn ** (2 * k) / math.factorial(2 * k) for k in range(7)]
    odd_terms = [(-1) ** k * turn ** (2 * k + 1) / math.factorial(2 * k + 1) for k in range(6)]
    square = rest * rest
    return sign * polynomial(square, even_terms), sign * rest * polynomial(square, odd_terms)


def both_parts(table):
    first = lax.broadcasted_iota(jnp.int32, (1, LANES), 1) < LANES // 2
    other = swapped(table)
    upper, lower = jnp.where(first, table, other), jnp.where(first, other, table)
    return jnp.concatenate([upper, lower], axis=0)


def half_rows(lane):
    row = lax.broadcasted_iota(jnp.int32, (BLK, LANES), 0)
    return row + jnp.where(lane >= LANES // 2, BLK, 0)


def phase_tables(rank, count, distance):
    lane = lax.broadcasted_iota(jnp.int32, (1, LANES), 1)
    kx = rank + ROWS * (lane // 8 % 8)
    kr = half_rows(lane) + ROWS * (lane % 8)
    fx = jnp.where(kx >= N // 2, kx - N, kx).astype(jnp.float32) * (1.0 / N)
    fr = jnp.where(kr >= N // 2, kr - N, kr).astype(jnp.float32) * (1.0 / N)
    cosine, sine = turn_tables(distance * jnp.sqrt((count + fr) ** 2 - 0.25 * fx**2))
    return both_parts(cosine), both_parts(sine)


def lane_rows(rank, starts_ref, choice_ref):
    lane = lax.broadcasted_iota(jnp.int32, (1, LANES), 1)
    row = lax.broadcasted_iota(jnp.int32, (16, LANES), 0)
    tile = rank // LANES * LANES
    own = lane == rank - tile
    spread = jnp.zeros((16, LANES), jnp.float32)
    for k in range(FEW):
        at = pl.multiple_of(tile + ROWS * k, LANES)
        some = starts_ref[:, pl.ds(at, LANES)].astype(jnp.float32)
        one = jnp.sum(jnp.where(own, some, 0.0), axis=1, keepdims=True)
        spread = jnp.where(lane // 8 % 8 == k, one, spread)
    starts, chosen = [], []
    for half in range(2):
        mine = jnp.where(row == 2 * (lane % 8) + half, spread, 0.0)
        starts.append(jnp.sum(mine, axis=0, keepdims=True).astype(jnp.int32))
        picked = jnp.zeros((1, LANES), jnp.float32)
        for j in range(FEW):
            at = 2 * j + half
            picked = jnp.where(lane % 8 == j, choice_ref[:1, at : at + 1], picked)
        chosen.append(picked.astype(jnp.int32))
    return starts, jnp.concatenate(chosen, axis=1)


PER_LANE = lax.GatherDimensionNumbers(
    offset_dims=(),
    collapsed_slice_dims=(0,),
    start_index_map=(0,),
    operand_batching_dims=(1,),
    start_indices_batching_dims=(1,),
)
PER_ROW = lax.GatherDimensionNumbers(
    offset_dims=(),
    collapsed_slice_dims=(1,),
    start_index_map=(1,),
    operand_batching_dims=(0,),
    start_indices_batching_dims=(0,),
)


def write_bands(coef_ref, high_ref, low_ref):
    coef = coef_ref[...]
    columns = jnp.transpose(jnp.concatenate([coef, coef], axis=0))
    lane = lax.broadcasted_iota(jnp.int32, (16, LANES), 1)
    row = lax.broadcasted_iota(jnp.int32, (16, LANES), 0)
    for d in range(NW):
        slope = BLK + STRETCH * d
        sloped = row * slope
        for g in range(BLK // 16):
            least = 16 * g * slope // BLK
            most = (16 * g + 15) * slope // BLK + TAPS - 1
            whole, rest = divmod(16 * g * slope, BLK)
            start = (sloped + rest) >> 7
            rows = pl.ds(d * BLK + 16 * g, 16)
            for tile in range(2):
                across = pl.ds(tile * LANES, LANES)
                if least >= (tile + 1) * LANES or most < tile * LANES:
                    high_ref[rows, across] = jnp.zeros((16, LANES), jnp.bfloat16)
                    low_ref[rows, across] = jnp.zeros((16, LANES), jnp.bfloat16)
                    continue
                ahead = (lane + (tile * LANES - whole)) - start
                tap = ahead & (TAPS - 1)
                taken = lax.gather(
                    columns[16 * g : 16 * g + 16],
                    (tap | (d * TAPS))[:, :, None],
                    PER_ROW,
                    (1, 1),
                    mode=lax.GatherScatterMode.PROMISE_IN_BOUNDS,
                )
                high, low = split(jnp.where(tap == ahead, taken, 0.0))
                high_ref[rows, across] = high
                low_ref[rows, across] = low


def stolt(turned, bh, bl, all_starts, chosen):
    lane = lax.broadcasted_iota(jnp.int32, (1, LANES), 1)
    following = jnp.where(lane % 8 == 7, 0.0, pltpu.roll(turned, LANES - 1, 1))
    long = jnp.concatenate([turned, following], axis=0)
    highs, lows = [], []
    for half in range(2):
        based = long[half * BLK : half * BLK + 3 * BLK]
        starts = all_starts[half]
        for bit in reversed(range(3, 8)):
            step = 1 << bit
            flagged = (starts >> bit) & 1 == 1
            moved = jnp.concatenate([based[step:], based[:step]], axis=0)
            based = jnp.where(flagged, moved, based)[: 2 * BLK + step]
        fine = lax.broadcasted_iota(jnp.int32, (8, LANES), 0) + (starts & 7)
        groups = [
            lax.gather(
                based[8 * g : 8 * g + 8],
                (fine & 7)[:, :, None],
                PER_LANE,
                (1, 1),
                mode=lax.GatherScatterMode.PROMISE_IN_BOUNDS,
            )
            for g in range(2 * BLK // 8 + 1)
        ]
        here = fine < 8
        based = jnp.concatenate(
            [jnp.where(here, groups[g], groups[g + 1]) for g in range(2 * BLK // 8)], axis=0
        )
        high, low = split(based)
        highs.append(high)
        lows.append(low)
    high, low = jnp.concatenate(highs, axis=1), jnp.concatenate(lows, axis=1)
    windows = jnp.concatenate([high, low, high], axis=0)
    result = jnp.zeros((BLK, 2 * LANES), jnp.float32)
    for d in range(NW):
        own = pl.ds(d * BLK, BLK)
        band = jnp.concatenate([bh[own, :], bh[own, :], bl[own, :]], axis=1)
        result = jnp.where(chosen == d, dot(band, windows), result)
    return jnp.concatenate([result[:, :LANES], result[:, LANES:]], axis=0)


def prepare_kernel(
    count_ref, distance_ref, choice_ref, starts_ref, coef_ref, phase_ref, bh, bl, lane_ref
):
    rank = own_rank()
    phase_ref[:ROWS], phase_ref[ROWS:] = phase_tables(rank, count_ref[0], distance_ref[0])
    write_bands(coef_ref, bh, bl)
    starts, chosen = lane_rows(rank, starts_ref, choice_ref)
    for half in range(2):
        lane_ref[half : half + 1, :] = starts[half]
        lane_ref[2 + half : 3 + half, :] = chosen[:, half * LANES : (half + 1) * LANES]
    lane_ref[4:8, :] = jnp.zeros((4, LANES), jnp.int32)


def range_kernel(x_ref, matrix_ref, turn_ref, phase_ref, bh, bl, lane_ref, out_ref):
    lines, side = forward(x_ref, matrix_ref, turn_ref, sides=True)
    turned = lines * phase_ref[:ROWS] + side * phase_ref[ROWS:]
    starts = [lane_ref[0:1, :], lane_ref[1:2, :]]
    chosen = jnp.concatenate([lane_ref[2:3, :], lane_ref[3:4, :]], axis=1)
    focused = stolt(turned, bh, bl, starts, chosen)
    inverse(focused, matrix_ref, turn_ref, out_ref)


VMEM = pl.BlockSpec(memory_space=pltpu.VMEM)
SMEM = pl.BlockSpec(memory_space=pltpu.SMEM)
HBM = pl.BlockSpec(memory_space=pltpu.HBM)
HELD = pltpu.VMEM((2, 2, 64, LANES), jnp.float32)


def call(kernel, shapes, *args, scalars=0, outs=VMEM, scratch=()):
    return pl.pallas_call(
        kernel,
        out_shape=shapes,
        in_specs=[SMEM] * scalars + [VMEM] * (len(args) - scalars),
        out_specs=[outs] * len(shapes) if isinstance(shapes, tuple) else outs,
        scratch_shapes=scratch,
        compiler_params=pltpu.CompilerParams(vmem_limit_bytes=32 * 2**20),
        cost_estimate=pl.CostEstimate(flops=10**10, bytes_accessed=2**20, transcendentals=0),
    )(*args)


def f32(*shape):
    return jax.ShapeDtypeStruct(shape, jnp.float32)


def bf16(*shape):
    return jax.ShapeDtypeStruct(shape, jnp.bfloat16)


def local(returns, center, distance, starts, choices, coefficients):
    whole = ("range", "pulse")
    known = tables()
    bands = bf16(NW * BLK, 2 * BLK)
    prepared = call(
        prepare_kernel,
        (f32(2 * ROWS, LANES), bands, bands, jax.ShapeDtypeStruct((8, LANES), jnp.int32)),
        center, distance, choices.astype(jnp.float32).reshape(1, 16), starts.T,
        coefficients.reshape(NW * TAPS, BLK),
        scalars=2,
    )
    x = call(pack_kernel, f32(32, 8, LANES), returns, scratch=[HELD])
    x = lax.all_to_all(x, "pulse", 0, 0, tiled=True)
    x = call(azimuth_kernel, f32(ROWS, LANES), x.reshape(ROWS, LANES), *known, prepared[-1])
    x = lax.all_to_all(x.reshape(ROWS, 1, LANES), whole, 0, 0, tiled=True)
    x = call(range_kernel, f32(ROWS, LANES), x.reshape(ROWS, LANES), *known, *prepared)
    x = lax.all_to_all(x.reshape(ROWS, 1, LANES), whole, 0, 0, tiled=True)
    x = call(azimuth_back_kernel, f32(ROWS, LANES), x.reshape(ROWS, LANES), *known)
    x = lax.all_to_all(x.reshape(32, 8, LANES), "pulse", 0, 0, tiled=True)
    return call(
        unpack_kernel, f32(2, 64, 256), x, outs=HBM,
        scratch=[HELD, pltpu.SemaphoreType.DMA((4,))],
    )


def solution(mesh):
    placed = (P(None, "pulse", "range"), P(), P(), P(), P(), P())
    return jax.shard_map(
        local, mesh=mesh, in_specs=placed, out_specs=P(None, "pulse", "range"), check_vma=False
    )
```

```python
import math

import jax
import jax.numpy as jnp
import ml_dtypes
import numpy as np
from jax import lax
from jax.experimental import pallas as pl
from jax.experimental.pallas import tpu as pltpu
from jax.sharding import PartitionSpec as P

BLK = 128
TAPS = 8
NW = 8
N = 2048
ROWS = 256
QUARTER = 64
FEW = 8
LANES = 128
STRETCH = (BLK - TAPS) // (NW - 1)


def halves(table):
    high = table.astype(np.float32).astype(ml_dtypes.bfloat16)
    low = (table - high.astype(np.float64)).astype(np.float32).astype(ml_dtypes.bfloat16)
    return high, low


FIRST, LAST = slice(0, 128), slice(128, 192)
INTO, INTO_I, BACK, BACK_I = (slice(at, at + 128) for at in range(192, 704, 128))


def tables():
    steps = np.arange(QUARTER)
    angle = 2.0 * math.pi / QUARTER * (steps[:, None] * steps[None, :] % QUARTER)
    cosine, sine = np.cos(angle), np.sin(angle)
    high, low = halves(np.concatenate([cosine, -sine]))
    first = np.concatenate([high, high, low, low], axis=1)
    last = np.concatenate(halves(np.concatenate([cosine, sine], axis=1)), axis=1)
    lane = np.arange(LANES)
    part, mid, low_digit = lane // 64, lane // 8 % 8, lane % 8
    eighth = 2.0 * math.pi / FEW * (mid[:, None] * low_digit[None, :] % FEW)
    cosine, sine = np.cos(eighth), np.sin(eighth)
    step = part[None, :] - part[:, None]
    few = np.where(step == 0, cosine, np.where(step > 0, -sine, sine))
    few = np.where(low_digit[:, None] == mid[None, :], few, 0.0)
    times_i = np.where(lane[:, None] % 64 == lane[None, :] % 64, step, 0).astype(np.float64)
    parts = []
    for one in (few, few @ times_i, few.T, few.T @ times_i):
        large = np.where(np.abs(one) > 0.9, np.round(one), 0.0)
        small = np.where(large == 0, np.sign(np.round(2 * one)), 0.0)
        parts.append(np.concatenate([large, small], axis=1))
    whole = [part.astype(ml_dtypes.bfloat16) for part in parts]
    matrices = np.concatenate([first, last, *whole])
    outer = 2.0 * math.pi / N * (np.arange(ROWS)[:, None] * mid[None, :])
    inner = np.concatenate([2.0 * math.pi / ROWS * steps * r for r in range(1, 4)])
    inner = np.broadcast_to(inner[:, None], (3 * QUARTER, LANES))
    turns = [np.cos(outer), np.sin(outer), np.cos(inner), np.sin(inner)]
    return matrices, np.concatenate(turns).astype(np.float32)


def split(x):
    high = x.astype(jnp.bfloat16)
    low = (x - high.astype(jnp.float32)).astype(jnp.bfloat16)
    return high, low


def dot(left, right):
    return jnp.dot(left, right, preferred_element_type=jnp.float32)


def swapped(x):
    return pltpu.roll(x, LANES // 2, 1)


def turned_by(pair, cosine, sine):
    a, b = pair
    return a * cosine + b * sine, b * cosine - a * sine


def butterfly(y):
    (a0, b0), (a1, b1), (a2, b2), (a3, b3) = y
    even, gap = (a0 + a2, b0 + b2), (a0 - a2, b0 - b2)
    odd, side = (a1 + a3, b1 + b3), (b1 - b3, a3 - a1)
    return [
        (even[0] + odd[0], even[1] + odd[1]),
        (gap[0] + side[0], gap[1] + side[1]),
        (even[0] - odd[0], even[1] - odd[1]),
        (gap[0] - side[0], gap[1] - side[1]),
    ]


def quarter_turns(y, turn_ref):
    found = [y[0]]
    for r in range(1, 4):
        cosine = turn_ref[pl.ds(2 * ROWS + (r - 1) * QUARTER, QUARTER)]
        sine = turn_ref[pl.ds(2 * ROWS + (r + 2) * QUARTER, QUARTER)]
        found.append(turned_by(y[r], cosine, sine))
    return found


def few_dft(x, table):
    both = dot(jnp.concatenate(x, axis=1), jnp.concatenate(table, axis=0))
    return both[:, :LANES] + both[:, LANES:] * math.sqrt(0.5)


def few_dft_both(x, table, table_i):
    table = jnp.concatenate([table, table_i], axis=1)
    both = dot(jnp.concatenate(x, axis=1), jnp.concatenate([table, table], axis=0))
    parts = [both[:, at * LANES : (at + 1) * LANES] for at in range(4)]
    return [parts[at] + parts[at + 1] * math.sqrt(0.5) for at in (0, 2)]


def forward(x_ref, matrix_ref, turn_ref, sides=False):
    x = jnp.concatenate([x_ref[pl.ds(r, QUARTER, stride=4), :] for r in range(4)], axis=1)
    high, low = split(x)
    both = dot(matrix_ref[FIRST], jnp.concatenate([high, low, high, low], axis=0))
    y = []
    for r in range(4):
        one = both[:, r * LANES : (r + 1) * LANES]
        y.append((one[:QUARTER], one[QUARTER:]))
    y = butterfly(quarter_turns(y, turn_ref))
    pair = [jnp.concatenate([one[at] for one in y], axis=0) for at in range(2)]
    a, b = turned_by(pair, turn_ref[:ROWS], turn_ref[ROWS : 2 * ROWS])
    into, into_i = matrix_ref[INTO], matrix_ref[INTO_I]
    if not sides:
        return few_dft([*split(a), *split(b)], [into, into, into_i, into_i])
    lane = lax.broadcasted_iota(jnp.int32, (1, LANES), 1)
    pieces = split(a + swapped(b * jnp.where(lane < LANES // 2, 1.0, -1.0)))
    return few_dft_both(pieces, into, into_i)


def inverse(x, matrix_ref, turn_ref, out_ref, scale=1.0):
    pieces = split(x)
    back, back_i = matrix_ref[BACK], matrix_ref[BACK_I]
    pair = few_dft_both(pieces, back, back_i)
    pair = turned_by(pair, turn_ref[:ROWS], turn_ref[ROWS : 2 * ROWS])
    y = [tuple(one[q * QUARTER : (q + 1) * QUARTER] for one in pair) for q in range(4)]
    y = quarter_turns(butterfly(y), turn_ref)
    y = jnp.concatenate([jnp.concatenate(one, axis=0) for one in y], axis=1)
    high, low = split(y)
    last = matrix_ref[LAST]
    wide = jnp.concatenate([last[:, :LANES], last[:, :LANES], last[:, LANES:]], axis=1)
    found = dot(wide, jnp.concatenate([high, low, high], axis=0))
    for r in range(4):
        one = found[:, r * LANES : (r + 1) * LANES]
        out_ref[pl.ds(r, QUARTER, stride=4), :] = one * scale


def exchange(parts):
    group = lax.broadcasted_iota(jnp.int32, parts[0].shape, 1) // 8
    parts = list(parts)
    for step in (1, 4):
        digit = group // step % 4
        masks = [digit == j for j in range(4)]
        for first in range(16):
            if first // step % 4:
                continue
            old = [parts[first + step * i] for i in range(4)]
            for i in range(4):
                one = old[i]
                for j in range(4):
                    if j != i:
                        moved = pltpu.roll(old[j], (j - i) * 8 * step % LANES, 1)
                        one = jnp.where(masks[j], moved, one)
                parts[first + step * i] = one
    return parts


def first_kernel(out_ref):
    out_ref[...] = jnp.zeros_like(out_ref)


def pack_kernel(count_ref, distance_ref, x_ref, first_ref, choice_ref, out_ref, held):
    for half in range(2):
        held[half] = x_ref[:, :, half * LANES : (half + 1) * LANES]
    parts = []
    for q in range(16):
        some = [held[half, q // 8, pl.ds(q % 8, 8, stride=8), :] for half in range(2)]
        parts.append(jnp.concatenate(some, axis=0))
    for g, one in enumerate(exchange(parts)):
        for half in range(2):
            out_ref[half * 16 + g] = one[half * 8 : half * 8 + 8]


def unpack_kernel(x_ref, out_ref, held, sems):
    parts = [jnp.concatenate([x_ref[g], x_ref[16 + g]], axis=0) for g in range(16)]
    copies = []
    for q, one in enumerate(exchange(parts)):
        for half in range(2):
            held[half, q // 8, pl.ds(q % 8, 8, stride=8), :] = one[half * 8 : half * 8 + 8]
        if q % 8 == 7:
            for half in range(2):
                copies.append(
                    pltpu.make_async_copy(
                        held.at[half, q // 8],
                        out_ref.at[q // 8, :, pl.ds(half * LANES, LANES)],
                        sems.at[q // 8 * 2 + half],
                    )
                )
                copies[-1].start()
    for copy in copies:
        copy.wait()


def azimuth_kernel(x_ref, matrix_ref, turn_ref, out_ref):
    out_ref[...] = forward(x_ref, matrix_ref, turn_ref)


def azimuth_back_kernel(x_ref, matrix_ref, turn_ref, out_ref):
    inverse(x_ref[...], matrix_ref, turn_ref, out_ref, 1.0 / (N * N))


def own_rank():
    return lax.axis_index("range") * 32 + lax.axis_index("pulse")


def polynomial(u, terms):
    total = jnp.full_like(u, terms[-1])
    for term in reversed(terms[:-1]):
        total = total * u + term
    return total


def turn_tables(turns):
    halves_count = jnp.round(2.0 * turns)
    rest = turns - 0.5 * halves_count
    odd = halves_count - 2.0 * jnp.floor(0.5 * halves_count)
    sign = 1.0 - 2.0 * odd
    turn = 2.0 * math.pi
    even_terms = [(-1) ** k * turn ** (2 * k) / math.factorial(2 * k) for k in range(7)]
    odd_terms = [(-1) ** k * turn ** (2 * k + 1) / math.factorial(2 * k + 1) for k in range(6)]
    square = rest * rest
    return sign * polynomial(square, even_terms), sign * rest * polynomial(square, odd_terms)


def both_parts(table):
    first = lax.broadcasted_iota(jnp.int32, (1, LANES), 1) < LANES // 2
    other = swapped(table)
    upper, lower = jnp.where(first, table, other), jnp.where(first, other, table)
    return jnp.concatenate([upper, lower], axis=0)


def half_rows(lane):
    row = lax.broadcasted_iota(jnp.int32, (BLK, LANES), 0)
    return row + jnp.where(lane >= LANES // 2, BLK, 0)


def phase_tables(rank, count, distance):
    lane = lax.broadcasted_iota(jnp.int32, (1, LANES), 1)
    kx = rank + ROWS * (lane // 8 % 8)
    kr = half_rows(lane) + ROWS * (lane % 8)
    fx = jnp.where(kx >= N // 2, kx - N, kx).astype(jnp.float32) * (1.0 / N)
    fr = jnp.where(kr >= N // 2, kr - N, kr).astype(jnp.float32) * (1.0 / N)
    cosine, sine = turn_tables(distance * jnp.sqrt((count + fr) ** 2 - 0.25 * fx**2))
    return both_parts(cosine), both_parts(sine)


def lane_rows(rank, starts_ref, choice_ref):
    lane = lax.broadcasted_iota(jnp.int32, (1, LANES), 1)
    row = lax.broadcasted_iota(jnp.int32, (16, LANES), 0)
    tile = rank // LANES * LANES
    own = lane == rank - tile
    spread = jnp.zeros((16, LANES), jnp.float32)
    for k in range(FEW):
        at = pl.multiple_of(tile + ROWS * k, LANES)
        some = starts_ref[:, pl.ds(at, LANES)].astype(jnp.float32)
        one = jnp.sum(jnp.where(own, some, 0.0), axis=1, keepdims=True)
        spread = jnp.where(lane // 8 % 8 == k, one, spread)
    starts, chosen = [], []
    for half in range(2):
        mine = jnp.where(row == 2 * (lane % 8) + half, spread, 0.0)
        starts.append(jnp.sum(mine, axis=0, keepdims=True).astype(jnp.int32))
        picked = jnp.zeros((1, LANES), jnp.float32)
        for j in range(FEW):
            at = 2 * j + half
            picked = jnp.where(lane % 8 == j, choice_ref[:1, at : at + 1], picked)
        chosen.append(picked.astype(jnp.int32))
    return starts, jnp.concatenate(chosen, axis=1)


PER_LANE = lax.GatherDimensionNumbers(
    offset_dims=(),
    collapsed_slice_dims=(0,),
    start_index_map=(0,),
    operand_batching_dims=(1,),
    start_indices_batching_dims=(1,),
)
PER_ROW = lax.GatherDimensionNumbers(
    offset_dims=(),
    collapsed_slice_dims=(1,),
    start_index_map=(1,),
    operand_batching_dims=(0,),
    start_indices_batching_dims=(0,),
)


def per_row(rows, at):
    return lax.gather(
        rows, at[:, :, None], PER_ROW, (1, 1), mode=lax.GatherScatterMode.PROMISE_IN_BOUNDS
    )


def write_bands(coef_ref, high_ref, low_ref):
    coef = coef_ref[...]
    columns = jnp.transpose(jnp.concatenate([coef, coef], axis=0))
    lane = lax.broadcasted_iota(jnp.int32, (8, LANES), 1)
    row = lax.broadcasted_iota(jnp.int32, (8, LANES), 0)
    slopes = BLK + STRETCH * ((lane >> 3) & (NW - 1))
    turned = []
    for first in range(0, BLK, 8):
        start = ((row + first) * slopes) >> 7
        at = (lane & -TAPS) | ((lane - start) & (TAPS - 1))
        turned.append(per_row(columns[first : first + 8], at))
    for d in range(NW):
        slope = BLK + STRETCH * d
        sloped = row * slope
        repeat = (lane & (TAPS - 1)) | (d * TAPS)
        for g in range(BLK // 16):
            pieces = [[], []]
            for first in (16 * g, 16 * g + 8):
                whole, rest = divmod(first * slope, BLK)
                most = (first + 7) * slope // BLK + TAPS - 1
                start = (sloped + rest) >> 7
                taken = per_row(turned[first // 8], repeat)
                for tile in range(2):
                    if whole >= (tile + 1) * LANES or most < tile * LANES:
                        pieces[tile].append(jnp.zeros((8, LANES), jnp.float32))
                        continue
                    ahead = (lane + (tile * LANES - whole)) - start
                    pieces[tile].append(jnp.where((ahead & -TAPS) == 0, taken, 0.0))
            rows = pl.ds(d * BLK + 16 * g, 16)
            for tile in range(2):
                across = pl.ds(tile * LANES, LANES)
                high, low = split(jnp.concatenate(pieces[tile], axis=0))
                high_ref[rows, across] = high
                low_ref[rows, across] = low


def stolt(turned, bh, bl, all_starts, chosen):
    lane = lax.broadcasted_iota(jnp.int32, (1, LANES), 1)
    following = jnp.where(lane % 8 == 7, 0.0, pltpu.roll(turned, LANES - 1, 1))
    long = jnp.concatenate([turned, following], axis=0)
    highs, lows = [], []
    for half in range(2):
        based = long[half * BLK : half * BLK + 3 * BLK]
        starts = all_starts[half]
        for bit in reversed(range(3, 8)):
            step = 1 << bit
            flagged = (starts >> bit) & 1 == 1
            moved = jnp.concatenate([based[step:], based[:step]], axis=0)
            based = jnp.where(flagged, moved, based)[: 2 * BLK + step]
        fine = lax.broadcasted_iota(jnp.int32, (8, LANES), 0) + (starts & 7)
        groups = [
            lax.gather(
                based[8 * g : 8 * g + 8],
                (fine & 7)[:, :, None],
                PER_LANE,
                (1, 1),
                mode=lax.GatherScatterMode.PROMISE_IN_BOUNDS,
            )
            for g in range(2 * BLK // 8 + 1)
        ]
        here = fine < 8
        based = jnp.concatenate(
            [jnp.where(here, groups[g], groups[g + 1]) for g in range(2 * BLK // 8)], axis=0
        )
        high, low = split(based)
        highs.append(high)
        lows.append(low)
    high, low = jnp.concatenate(highs, axis=1), jnp.concatenate(lows, axis=1)
    windows = jnp.concatenate([high, low, high], axis=0)
    result = jnp.zeros((BLK, 2 * LANES), jnp.float32)
    for d in range(NW):
        own = pl.ds(d * BLK, BLK)
        band = jnp.concatenate([bh[own, :], bh[own, :], bl[own, :]], axis=1)
        result = jnp.where(chosen == d, dot(band, windows), result)
    return jnp.concatenate([result[:, :LANES], result[:, LANES:]], axis=0)


def range_kernel(
    count_ref, distance_ref, x_ref, matrix_ref, turn_ref, choice_ref, starts_ref, coef_ref,
    out_ref, bh, bl,
):
    rank = own_rank()
    lines, side = forward(x_ref, matrix_ref, turn_ref, sides=True)
    cosine, sine = phase_tables(rank, count_ref[0], distance_ref[0])
    turned = lines * cosine + side * sine
    write_bands(coef_ref, bh, bl)
    starts, chosen = lane_rows(rank, starts_ref, choice_ref)
    focused = stolt(turned, bh, bl, starts, chosen)
    inverse(focused, matrix_ref, turn_ref, out_ref)


VMEM = pl.BlockSpec(memory_space=pltpu.VMEM)
SMEM = pl.BlockSpec(memory_space=pltpu.SMEM)
HBM = pl.BlockSpec(memory_space=pltpu.HBM)
HELD = pltpu.VMEM((2, 2, 64, LANES), jnp.float32)


def call(kernel, shapes, *args, scalars=0, outs=VMEM, scratch=()):
    return pl.pallas_call(
        kernel,
        out_shape=shapes,
        in_specs=[SMEM] * scalars + [VMEM] * (len(args) - scalars),
        out_specs=jax.tree.map(lambda _: outs, shapes),
        scratch_shapes=scratch,
        compiler_params=pltpu.CompilerParams(vmem_limit_bytes=32 * 2**20),
        cost_estimate=pl.CostEstimate(flops=10**10, bytes_accessed=2**20, transcendentals=0),
    )(*args)


def f32(*shape):
    return jax.ShapeDtypeStruct(shape, jnp.float32)


def bf16(*shape):
    return jax.ShapeDtypeStruct(shape, jnp.bfloat16)


def local(returns, center, distance, starts, choices, coefficients):
    whole = ("range", "pulse")
    known = tables()
    choices = choices.astype(jnp.float32).reshape(1, 16)
    first = call(first_kernel, f32(8, LANES))
    x = call(
        pack_kernel, f32(32, 8, LANES), center, distance, returns, first, choices,
        scalars=2, scratch=[HELD],
    )
    x = lax.all_to_all(x, "pulse", 0, 0, tiled=True)
    x = call(azimuth_kernel, f32(ROWS, LANES), x.reshape(ROWS, LANES), *known)
    x = lax.all_to_all(x.reshape(ROWS, 1, LANES), whole, 0, 0, tiled=True)
    x = call(
        range_kernel, f32(ROWS, LANES), center, distance, x.reshape(ROWS, LANES), *known,
        choices, starts.T, coefficients.reshape(NW * TAPS, BLK),
        scalars=2,
        scratch=[pltpu.VMEM((NW * BLK, 2 * BLK), jnp.bfloat16)] * 2,
    )
    x = lax.all_to_all(x.reshape(ROWS, 1, LANES), whole, 0, 0, tiled=True)
    x = call(azimuth_back_kernel, f32(ROWS, LANES), x.reshape(ROWS, LANES), *known)
    x = lax.all_to_all(x.reshape(32, 8, LANES), "pulse", 0, 0, tiled=True)
    return call(
        unpack_kernel, f32(2, 64, 256), x, outs=HBM,
        scratch=[HELD, pltpu.SemaphoreType.DMA((4,))],
    )


def solution(mesh):
    placed = (P(None, "pulse", "range"), P(), P(), P(), P(), P())
    return jax.shard_map(
        local, mesh=mesh, in_specs=placed, out_specs=P(None, "pulse", "range"), check_vma=False
    )
```

```python
import math

import jax
import jax.numpy as jnp
import ml_dtypes
import numpy as np
from jax import lax
from jax.experimental import pallas as pl
from jax.experimental.pallas import tpu as pltpu
from jax.sharding import PartitionSpec as P

BLK = 128
TAPS = 8
NW = 8
N = 2048
ROWS = 256
QUARTER = 64
FEW = 8
LANES = 128
STRETCH = (BLK - TAPS) // (NW - 1)


def halves(table):
    high = table.astype(np.float32).astype(ml_dtypes.bfloat16)
    low = (table - high.astype(np.float64)).astype(np.float32).astype(ml_dtypes.bfloat16)
    return high, low


FIRST, LAST = slice(0, 128), slice(128, 192)
INTO, INTO_I, BACK, BACK_I = (slice(at, at + 128) for at in range(192, 704, 128))


def tables():
    steps = np.arange(QUARTER)
    angle = 2.0 * math.pi / QUARTER * (steps[:, None] * steps[None, :] % QUARTER)
    cosine, sine = np.cos(angle), np.sin(angle)
    high, low = halves(np.concatenate([cosine, -sine]))
    first = np.concatenate([high, high, low, low], axis=1)
    last = np.concatenate(halves(np.concatenate([cosine, sine], axis=1)), axis=1)
    lane = np.arange(LANES)
    part, mid, low_digit = lane // 64, lane // 8 % 8, lane % 8
    eighth = 2.0 * math.pi / FEW * (mid[:, None] * low_digit[None, :] % FEW)
    cosine, sine = np.cos(eighth), np.sin(eighth)
    step = part[None, :] - part[:, None]
    few = np.where(step == 0, cosine, np.where(step > 0, -sine, sine))
    few = np.where(low_digit[:, None] == mid[None, :], few, 0.0)
    times_i = np.where(lane[:, None] % 64 == lane[None, :] % 64, step, 0).astype(np.float64)
    parts = []
    for one in (few, few @ times_i, few.T, few.T @ times_i):
        large = np.where(np.abs(one) > 0.9, np.round(one), 0.0)
        small = np.where(large == 0, np.sign(np.round(2 * one)), 0.0)
        parts.append(np.concatenate([large, small], axis=1))
    whole = [part.astype(ml_dtypes.bfloat16) for part in parts]
    matrices = np.concatenate([first, last, *whole])
    outer = 2.0 * math.pi / N * (np.arange(ROWS)[:, None] * mid[None, :])
    inner = np.concatenate([2.0 * math.pi / ROWS * steps * r for r in range(1, 4)])
    inner = np.broadcast_to(inner[:, None], (3 * QUARTER, LANES))
    turns = [np.cos(outer), np.sin(outer), np.cos(inner), np.sin(inner)]
    return matrices, np.concatenate(turns).astype(np.float32)


def split(x):
    high = x.astype(jnp.bfloat16)
    low = (x - high.astype(jnp.float32)).astype(jnp.bfloat16)
    return high, low


def dot(left, right):
    return jnp.dot(left, right, preferred_element_type=jnp.float32)


def swapped(x):
    return pltpu.roll(x, LANES // 2, 1)


def turned_by(pair, cosine, sine):
    a, b = pair
    return a * cosine + b * sine, b * cosine - a * sine


def butterfly(y):
    (a0, b0), (a1, b1), (a2, b2), (a3, b3) = y
    even, gap = (a0 + a2, b0 + b2), (a0 - a2, b0 - b2)
    odd, side = (a1 + a3, b1 + b3), (b1 - b3, a3 - a1)
    return [
        (even[0] + odd[0], even[1] + odd[1]),
        (gap[0] + side[0], gap[1] + side[1]),
        (even[0] - odd[0], even[1] - odd[1]),
        (gap[0] - side[0], gap[1] - side[1]),
    ]


def quarter_turns(y, turn_ref):
    found = [y[0]]
    for r in range(1, 4):
        cosine = turn_ref[pl.ds(2 * ROWS + (r - 1) * QUARTER, QUARTER)]
        sine = turn_ref[pl.ds(2 * ROWS + (r + 2) * QUARTER, QUARTER)]
        found.append(turned_by(y[r], cosine, sine))
    return found


def few_dft(x, table):
    both = dot(jnp.concatenate(x, axis=1), jnp.concatenate(table, axis=0))
    return both[:, :LANES] + both[:, LANES:] * math.sqrt(0.5)


def few_dft_both(x, table, table_i):
    table = jnp.concatenate([table, table_i], axis=1)
    both = dot(jnp.concatenate(x, axis=1), jnp.concatenate([table, table], axis=0))
    parts = [both[:, at * LANES : (at + 1) * LANES] for at in range(4)]
    return [parts[at] + parts[at + 1] * math.sqrt(0.5) for at in (0, 2)]


def forward(x_ref, matrix_ref, turn_ref, sides=False):
    x = jnp.concatenate([x_ref[pl.ds(r, QUARTER, stride=4), :] for r in range(4)], axis=1)
    high, low = split(x)
    both = dot(matrix_ref[FIRST], jnp.concatenate([high, low, high, low], axis=0))
    y = []
    for r in range(4):
        one = both[:, r * LANES : (r + 1) * LANES]
        y.append((one[:QUARTER], one[QUARTER:]))
    y = butterfly(quarter_turns(y, turn_ref))
    pair = [jnp.concatenate([one[at] for one in y], axis=0) for at in range(2)]
    a, b = turned_by(pair, turn_ref[:ROWS], turn_ref[ROWS : 2 * ROWS])
    into, into_i = matrix_ref[INTO], matrix_ref[INTO_I]
    if not sides:
        return few_dft([*split(a), *split(b)], [into, into, into_i, into_i])
    pieces = [*split(a), *split(b)]
    table = jnp.concatenate([into, into, into_i, into_i], axis=0)
    table_i = jnp.concatenate([into_i, into_i, -into, -into], axis=0)
    both = dot(jnp.concatenate(pieces, axis=1), jnp.concatenate([table, table_i], axis=1))
    parts = [both[:, at * LANES : (at + 1) * LANES] for at in range(4)]
    return [parts[at] + parts[at + 1] * math.sqrt(0.5) for at in (0, 2)]


def inverse(x, matrix_ref, turn_ref, out_ref, scale=1.0):
    pieces = split(x)
    back, back_i = matrix_ref[BACK], matrix_ref[BACK_I]
    pair = few_dft_both(pieces, back, back_i)
    pair = turned_by(pair, turn_ref[:ROWS], turn_ref[ROWS : 2 * ROWS])
    y = [tuple(one[q * QUARTER : (q + 1) * QUARTER] for one in pair) for q in range(4)]
    y = quarter_turns(butterfly(y), turn_ref)
    y = jnp.concatenate([jnp.concatenate(one, axis=0) for one in y], axis=1)
    high, low = split(y)
    last = matrix_ref[LAST]
    wide = jnp.concatenate([last[:, :LANES], last[:, :LANES], last[:, LANES:]], axis=1)
    found = dot(wide, jnp.concatenate([high, low, high], axis=0))
    for r in range(4):
        one = found[:, r * LANES : (r + 1) * LANES]
        out_ref[pl.ds(r, QUARTER, stride=4), :] = one * scale


def exchange(parts):
    group = lax.broadcasted_iota(jnp.int32, parts[0].shape, 1) // 8
    parts = list(parts)
    for step in (1, 4):
        digit = group // step % 4
        masks = [digit == j for j in range(4)]
        for first in range(16):
            if first // step % 4:
                continue
            old = [parts[first + step * i] for i in range(4)]
            for i in range(4):
                one = old[i]
                for j in range(4):
                    if j != i:
                        moved = pltpu.roll(old[j], (j - i) * 8 * step % LANES, 1)
                        one = jnp.where(masks[j], moved, one)
                parts[first + step * i] = one
    return parts


def first_kernel(out_ref):
    out_ref[...] = jnp.zeros_like(out_ref)


def pack_kernel(count_ref, distance_ref, x_ref, first_ref, choice_ref, out_ref, held):
    for half in range(2):
        held[half] = x_ref[:, :, half * LANES : (half + 1) * LANES]
    parts = []
    for q in range(16):
        some = [held[half, q // 8, pl.ds(q % 8, 8, stride=8), :] for half in range(2)]
        parts.append(jnp.concatenate(some, axis=0))
    for g, one in enumerate(exchange(parts)):
        for half in range(2):
            out_ref[half * 16 + g] = one[half * 8 : half * 8 + 8]


def unpack_kernel(x_ref, out_ref, held, sems):
    parts = [jnp.concatenate([x_ref[g], x_ref[16 + g]], axis=0) for g in range(16)]
    copies = []
    for q, one in enumerate(exchange(parts)):
        for half in range(2):
            held[half, q // 8, pl.ds(q % 8, 8, stride=8), :] = one[half * 8 : half * 8 + 8]
        if q % 8 == 7:
            for half in range(2):
                copies.append(
                    pltpu.make_async_copy(
                        held.at[half, q // 8],
                        out_ref.at[q // 8, :, pl.ds(half * LANES, LANES)],
                        sems.at[q // 8 * 2 + half],
                    )
                )
                copies[-1].start()
    for copy in copies:
        copy.wait()


def azimuth_kernel(x_ref, matrix_ref, turn_ref, out_ref):
    out_ref[...] = forward(x_ref, matrix_ref, turn_ref)


def azimuth_back_kernel(x_ref, matrix_ref, turn_ref, out_ref):
    inverse(x_ref[...], matrix_ref, turn_ref, out_ref, 1.0 / (N * N))


def own_rank():
    return lax.axis_index("range") * 32 + lax.axis_index("pulse")


def polynomial(u, terms):
    total = jnp.full_like(u, terms[-1])
    for term in reversed(terms[:-1]):
        total = total * u + term
    return total


def turn_tables(turns):
    halves_count = jnp.round(2.0 * turns)
    rest = turns - 0.5 * halves_count
    odd = halves_count - 2.0 * jnp.floor(0.5 * halves_count)
    sign = 1.0 - 2.0 * odd
    turn = 2.0 * math.pi
    even_terms = [(-1) ** k * turn ** (2 * k) / math.factorial(2 * k) for k in range(7)]
    odd_terms = [(-1) ** k * turn ** (2 * k + 1) / math.factorial(2 * k + 1) for k in range(6)]
    square = rest * rest
    return sign * polynomial(square, even_terms), sign * rest * polynomial(square, odd_terms)


def both_parts(table):
    first = lax.broadcasted_iota(jnp.int32, (1, LANES), 1) < LANES // 2
    other = swapped(table)
    upper, lower = jnp.where(first, table, other), jnp.where(first, other, table)
    return jnp.concatenate([upper, lower], axis=0)


def half_rows(lane):
    row = lax.broadcasted_iota(jnp.int32, (BLK, LANES), 0)
    return row + jnp.where(lane >= LANES // 2, BLK, 0)


def phase_tables(rank, count, distance):
    lane = lax.broadcasted_iota(jnp.int32, (1, LANES), 1)
    kx = rank + ROWS * (lane // 8 % 8)
    kr = half_rows(lane) + ROWS * (lane % 8)
    fx = jnp.where(kx >= N // 2, kx - N, kx).astype(jnp.float32) * (1.0 / N)
    fr = jnp.where(kr >= N // 2, kr - N, kr).astype(jnp.float32) * (1.0 / N)
    cosine, sine = turn_tables(distance * jnp.sqrt((count + fr) ** 2 - 0.25 * fx**2))
    return both_parts(cosine), both_parts(sine)


def lane_rows(rank, starts_ref, choice_ref):
    lane = lax.broadcasted_iota(jnp.int32, (1, LANES), 1)
    row = lax.broadcasted_iota(jnp.int32, (16, LANES), 0)
    tile = rank // LANES * LANES
    own = lane == rank - tile
    spread = jnp.zeros((16, LANES), jnp.float32)
    for k in range(FEW):
        at = pl.multiple_of(tile + ROWS * k, LANES)
        some = starts_ref[:, pl.ds(at, LANES)].astype(jnp.float32)
        one = jnp.sum(jnp.where(own, some, 0.0), axis=1, keepdims=True)
        spread = jnp.where(lane // 8 % 8 == k, one, spread)
    starts, chosen = [], []
    for half in range(2):
        mine = jnp.where(row == 2 * (lane % 8) + half, spread, 0.0)
        starts.append(jnp.sum(mine, axis=0, keepdims=True).astype(jnp.int32))
        picked = jnp.zeros((1, LANES), jnp.float32)
        for j in range(FEW):
            at = 2 * j + half
            picked = jnp.where(lane % 8 == j, choice_ref[:1, at : at + 1], picked)
        chosen.append(picked.astype(jnp.int32))
    return starts, jnp.concatenate(chosen, axis=1)


PER_LANE = lax.GatherDimensionNumbers(
    offset_dims=(),
    collapsed_slice_dims=(0,),
    start_index_map=(0,),
    operand_batching_dims=(1,),
    start_indices_batching_dims=(1,),
)
PER_ROW = lax.GatherDimensionNumbers(
    offset_dims=(),
    collapsed_slice_dims=(1,),
    start_index_map=(1,),
    operand_batching_dims=(0,),
    start_indices_batching_dims=(0,),
)


def per_row(rows, at):
    return lax.gather(
        rows, at[:, :, None], PER_ROW, (1, 1), mode=lax.GatherScatterMode.PROMISE_IN_BOUNDS
    )


def write_bands(coef_ref, high_ref, low_ref):
    coef = coef_ref[...]
    columns = jnp.transpose(jnp.concatenate([coef, coef], axis=0))
    lane = lax.broadcasted_iota(jnp.int32, (8, LANES), 1)
    row = lax.broadcasted_iota(jnp.int32, (8, LANES), 0)
    slopes = BLK + STRETCH * ((lane >> 3) & (NW - 1))
    turned = []
    for first in range(0, BLK, 8):
        start = ((row + first) * slopes) >> 7
        at = (lane & -TAPS) | ((lane - start) & (TAPS - 1))
        turned.append(per_row(columns[first : first + 8], at))
    for d in range(NW):
        slope = BLK + STRETCH * d
        sloped = row * slope
        repeat = (lane & (TAPS - 1)) | (d * TAPS)
        for g in range(BLK // 16):
            pieces = [[], []]
            for first in (16 * g, 16 * g + 8):
                whole, rest = divmod(first * slope, BLK)
                most = (first + 7) * slope // BLK + TAPS - 1
                start = (sloped + rest) >> 7
                taken = per_row(turned[first // 8], repeat)
                for tile in range(2):
                    if whole >= (tile + 1) * LANES or most < tile * LANES:
                        pieces[tile].append(jnp.zeros((8, LANES), jnp.float32))
                        continue
                    ahead = (lane + (tile * LANES - whole)) - start
                    pieces[tile].append(jnp.where((ahead & -TAPS) == 0, taken, 0.0))
            rows = pl.ds(d * BLK + 16 * g, 16)
            for tile in range(2):
                across = pl.ds(tile * LANES, LANES)
                high, low = split(jnp.concatenate(pieces[tile], axis=0))
                high_ref[rows, across] = high
                low_ref[rows, across] = low


def stolt(turned, bh, bl, all_starts, chosen):
    lane = lax.broadcasted_iota(jnp.int32, (1, LANES), 1)
    following = jnp.where(lane % 8 == 7, 0.0, pltpu.roll(turned, LANES - 1, 1))
    long = jnp.concatenate([turned, following], axis=0)
    highs, lows = [], []
    for half in range(2):
        based = long[half * BLK : half * BLK + 3 * BLK]
        starts = all_starts[half]
        for bit in reversed(range(3, 8)):
            step = 1 << bit
            flagged = (starts >> bit) & 1 == 1
            moved = jnp.concatenate([based[step:], based[:step]], axis=0)
            based = jnp.where(flagged, moved, based)[: 2 * BLK + step]
        fine = lax.broadcasted_iota(jnp.int32, (8, LANES), 0) + (starts & 7)
        groups = [
            lax.gather(
                based[8 * g : 8 * g + 8],
                (fine & 7)[:, :, None],
                PER_LANE,
                (1, 1),
                mode=lax.GatherScatterMode.PROMISE_IN_BOUNDS,
            )
            for g in range(2 * BLK // 8 + 1)
        ]
        here = fine < 8
        based = jnp.concatenate(
            [jnp.where(here, groups[g], groups[g + 1]) for g in range(2 * BLK // 8)], axis=0
        )
        high, low = split(based)
        highs.append(high)
        lows.append(low)
    high, low = jnp.concatenate(highs, axis=1), jnp.concatenate(lows, axis=1)
    windows = jnp.concatenate([high, low, high], axis=0)
    result = jnp.zeros((BLK, 2 * LANES), jnp.float32)
    for d in range(NW):
        own = pl.ds(d * BLK, BLK)
        band = jnp.concatenate([bh[own, :], bh[own, :], bl[own, :]], axis=1)
        result = jnp.where(chosen == d, dot(band, windows), result)
    return jnp.concatenate([result[:, :LANES], result[:, LANES:]], axis=0)


def range_kernel(
    count_ref, distance_ref, x_ref, matrix_ref, turn_ref, choice_ref, starts_ref, coef_ref,
    out_ref, bh, bl,
):
    rank = own_rank()
    lines, side = forward(x_ref, matrix_ref, turn_ref, sides=True)
    cosine, sine = phase_tables(rank, count_ref[0], distance_ref[0])
    turned = lines * cosine + side * sine
    write_bands(coef_ref, bh, bl)
    starts, chosen = lane_rows(rank, starts_ref, choice_ref)
    focused = stolt(turned, bh, bl, starts, chosen)
    inverse(focused, matrix_ref, turn_ref, out_ref)


VMEM = pl.BlockSpec(memory_space=pltpu.VMEM)
SMEM = pl.BlockSpec(memory_space=pltpu.SMEM)
HBM = pl.BlockSpec(memory_space=pltpu.HBM)
HELD = pltpu.VMEM((2, 2, 64, LANES), jnp.float32)


def call(kernel, shapes, *args, scalars=0, outs=VMEM, scratch=()):
    return pl.pallas_call(
        kernel,
        out_shape=shapes,
        in_specs=[SMEM] * scalars + [VMEM] * (len(args) - scalars),
        out_specs=jax.tree.map(lambda _: outs, shapes),
        scratch_shapes=scratch,
        compiler_params=pltpu.CompilerParams(vmem_limit_bytes=32 * 2**20),
        cost_estimate=pl.CostEstimate(flops=10**10, bytes_accessed=2**20, transcendentals=0),
    )(*args)


def f32(*shape):
    return jax.ShapeDtypeStruct(shape, jnp.float32)


def bf16(*shape):
    return jax.ShapeDtypeStruct(shape, jnp.bfloat16)


def local(returns, center, distance, starts, choices, coefficients):
    whole = ("range", "pulse")
    known = tables()
    choices = choices.astype(jnp.float32).reshape(1, 16)
    first = call(first_kernel, f32(8, LANES))
    x = call(
        pack_kernel, f32(32, 8, LANES), center, distance, returns, first, choices,
        scalars=2, scratch=[HELD],
    )
    x = lax.all_to_all(x, "pulse", 0, 0, tiled=True)
    x = call(azimuth_kernel, f32(ROWS, LANES), x.reshape(ROWS, LANES), *known)
    x = lax.all_to_all(x.reshape(ROWS, 1, LANES), whole, 0, 0, tiled=True)
    x = call(
        range_kernel, f32(ROWS, LANES), center, distance, x.reshape(ROWS, LANES), *known,
        choices, starts.T, coefficients.reshape(NW * TAPS, BLK),
        scalars=2,
        scratch=[pltpu.VMEM((NW * BLK, 2 * BLK), jnp.bfloat16)] * 2,
    )
    x = lax.all_to_all(x.reshape(ROWS, 1, LANES), whole, 0, 0, tiled=True)
    x = call(azimuth_back_kernel, f32(ROWS, LANES), x.reshape(ROWS, LANES), *known)
    x = lax.all_to_all(x.reshape(32, 8, LANES), "pulse", 0, 0, tiled=True)
    return call(
        unpack_kernel, f32(2, 64, 256), x, outs=HBM,
        scratch=[HELD, pltpu.SemaphoreType.DMA((4,))],
    )


def solution(mesh):
    placed = (P(None, "pulse", "range"), P(), P(), P(), P(), P())
    return jax.shard_map(
        local, mesh=mesh, in_specs=placed, out_specs=P(None, "pulse", "range"), check_vma=False
    )
```
